32 devices in a mesh: member: 2 (over y), lat: 4 (over z), lon: 2 (over x), ch: 2 (over core).
Axes of the slice: x: 2, y: 2, z: 4, core: 2. Of those that a mesh axis runs over, the one named last changes fastest.
Arguments:
- grid_latent: bfloat16 [16384, 512], P(('member', 'lat', 'lon', 'ch')), parts along dimension 0, may hold values from -6 to 6
- grid_owner: int32 [16384, 1], P(('member', 'lat', 'lon', 'ch')), parts along dimension 0, may hold values from 0 to 7; in each aligned block of 512 rows (0 to 511, 512 to 1023, ...) at most 128 rows name the same one
- grid_target: int32 [16384, 2], P(('member', 'lat', 'lon', 'ch')), parts along dimension 0, may hold values from 0 to 255
- mesh_latent: bfloat16 [8192, 512], P(('member', 'lat', 'lon', 'ch')), parts along dimension 0, may hold values from -6 to 6
- edge_latent: bfloat16 [16384, 512], P(('member', 'lat', 'lon', 'ch')), parts along dimension 0, may hold values from -6 to 6
- mesh_sender: int32 [16384], P(('member', 'lat', 'lon', 'ch')), parts along dimension 0, may hold values from 0 to 511
- mesh_receiver: int32 [16384], P(('member', 'lat', 'lon', 'ch')), parts along dimension 0, may hold values from 0 to 255
- halo_rows: int32 [2048], P(('member', 'lat', 'lon', 'ch')), parts along dimension 0, may hold values from 0 to 255
- weights: bfloat16 [13, 512, 512], P(None, 'ch'), may hold values from -0.25 to 0.25
- biases: float32 [4, 512], replicated, may hold values from -3 to 3
- gains: float32 [4, 512], replicated, may hold values from 0.5 to 1.5
Outputs:
- mesh_out: bfloat16 [8192, 512], P(('member', 'lat', 'lon', 'ch')), parts along dimension 0
The draws below stay inside these ranges and needn't reach their ends.
There are 2 independent parts, one for each index of `member`. The reference program is written for one: setup_inputs(seed, part) draws one part's arguments, and reference() takes and returns one part's arrays. A program takes and returns all parts, laid end to end along the dimension named above; an argument that names none is the same for every part. Nothing has to cross between parts.
Inputs may be any that keep to these rules, and one draw needn't show every extreme that they name: `grid_owner`: among the rows of one device, no owner is named by more than 128 rows, and in every draw some device names some owner exactly 128 times. `mesh_sender`: entries 256 + p * 64 + i name entry i of the lent list of neighbour p.
All inputs are finite; a program needn't handle non-finite values.
Results may differ from the reference program's by a relative error of at most 0.008.
Values may be sent and summed in bfloat16 or wider, within the bound.
No kernel may reach another device: no remote copies, remote signals or barrier semaphores. Data moves between devices by JAX's collectives and lax.ppermute only.
A program may use at most 128 MiB of HBM per device.

```python
import math
import jax
import jax.numpy as jnp
import numpy as np
from jax import lax

D = 512
G_DEV = 512
M_DEV = 256
E_DEV = 512
H_DEV = 64
CAP = 128
GRID = 8192
MESH = 4096
EDGES = 8192
HALO = 1024
N_LAT = 4
N_LON = 2
N_CH = 2


def with_ends(drawn, rng, least, top_value):
    spot = [jax.random.randint(jax.random.fold_in(rng, axis), (), 0, length) for axis, length in enumerate(drawn.shape)]
    widest = drawn.shape.index(max(drawn.shape))
    beside = spot[:widest] + [(spot[widest] + 1) % drawn.shape[widest]] + spot[widest + 1:]
    return drawn.at[tuple(spot)].set(least).at[tuple(beside)].set(top_value)


def block_levels(stream_key, dims, pieces, least, high):
    def one(dim, blocks):
        draws = jax.random.uniform(jax.random.fold_in(jax.random.fold_in(stream_key, 6), dim), (blocks,), jnp.float32, least / len(pieces), high / len(pieces))
        return jnp.repeat(jnp.exp(draws), dims[dim] // blocks).reshape((-1,) + (1,) * (len(dims) - dim - 1))

    loudness = one(*pieces[0])
    for cut in pieces[1:]:
        loudness = loudness * one(*cut)
    return loudness


def routed_block(key, own, number, rows, count, top, reach, lean):
    ranking = jax.random.permutation(key, count)
    heavy_load, usual = load_shares(count, rows * top, reach, lean, True), load_shares(count, rows * top, reach, lean, False)
    places = jnp.arange(count)

    def named(tallies, turn):
        used = int((tallies > 0).sum())
        fixed = max(1, used // 4)
        shifted = fixed + (places - fixed + turn * (used - fixed)) % max(1, count - fixed)
        return jnp.zeros((count,), jnp.int32).at[ranking[jnp.where(places < fixed, places, shifted)]].set(jnp.asarray(tallies, jnp.int32))

    tallies = jnp.where(number % 4 == 0, named(heavy_load, number // 4), named(usual, number - number // 4 - 1))
    mixed = jax.random.permutation(jax.random.fold_in(own, 3), count)
    giver, taker = mixed[0:count // 2 * 2:2], mixed[1:count // 2 * 2:2]
    slack = jnp.minimum(tallies[giver] - 1, reach - tallies[taker]) // 2
    slack = jnp.where((giver == ranking[0]) | (taker == ranking[0]) | (tallies[taker] == 0), 0, jnp.maximum(slack, 0))
    shifted = jax.random.randint(jax.random.fold_in(own, 4), (count // 2,), 0, 1 << 20) % (slack + 1)
    tallies = tallies.at[giver].add(-shifted).at[taker].add(shifted)
    items = jnp.searchsorted(jnp.cumsum(tallies), jnp.arange(rows * top), side="right").astype(jnp.int32)
    table = items.reshape(top, rows).T
    table = table[jax.random.permutation(jax.random.fold_in(own, 1), rows)]
    turn = jax.random.randint(jax.random.fold_in(own, 2), (rows, 1), 0, top)
    return jnp.take_along_axis(table, (jnp.arange(top)[None, :] + turn) % top, axis=1)


def load_shares(amount, total, limit, lean, full):
    weights = [(1 << 20) // math.isqrt(grade ** lean) + 1 for grade in range(1, amount + 1)]
    largest = limit if full else min(limit, max(-(-total // amount), total * weights[0] // sum(weights)))
    least = 1 if total - largest >= amount - 1 else 0
    counts, surplus = [largest] + [least] * (amount - 1), total - largest - least * (amount - 1)
    while surplus > 0:
        candidates = [i for i in range(1, amount) if counts[i] < largest] or [i for i in range(1, amount) if counts[i] < limit]
        mass, budget = sum([weights[i] for i in candidates]), surplus
        for i in candidates:
            extra = min(limit - counts[i], max(1, budget * weights[i] // mass), surplus)
            counts[i] = counts[i] + extra
            surplus = surplus - extra
    return np.array(counts)


def gaussian(own_key, shape, deviation, bound, cuts=(), held_as=jnp.bfloat16):
    gain = block_levels(own_key, shape, cuts, -0.22, 0.18) if cuts else 1.0
    drawn = jax.random.normal(own_key, shape, jnp.float32) * deviation * gain
    return jnp.minimum(jnp.maximum(drawn, -bound), bound).astype(held_as)


def setup_inputs(seed: int = 0, part: int = 0) -> dict:
    splits = jax.random.split(jax.random.key(seed), 12)
    part_keys = jax.random.split(jax.random.fold_in(splits[11], part), 12)
    grid_latent = gaussian(part_keys[0], (GRID, D), 1.0, 6.0, ((0, 16),))
    grid_owner_keys = jax.random.split(jax.random.fold_in(part_keys[1], 1), GRID // G_DEV)
    grid_owner_turns = jax.random.permutation(jax.random.fold_in(part_keys[1], 3), GRID // G_DEV)
    grid_owner = jax.vmap(lambda own, number: routed_block(jax.random.fold_in(part_keys[1], 2), own, number, G_DEV, N_LAT * N_LON, 1, CAP, 2))(grid_owner_keys, grid_owner_turns).reshape((GRID, 1))
    grid_target = with_ends(jax.random.randint(part_keys[2], (GRID, 2), 0, M_DEV), jax.random.fold_in(part_keys[2], 1), 0, M_DEV - 1).astype(jnp.int32)
    mesh_latent = gaussian(part_keys[3], (MESH, D), 1.0, 6.0, ((0, 16),))
    edge_latent = gaussian(part_keys[4], (EDGES, D), 1.0, 6.0, ((0, 16),))
    mesh_sender = with_ends(jax.random.randint(part_keys[5], (EDGES,), 0, M_DEV + 4 * H_DEV), jax.random.fold_in(part_keys[5], 1), 0, (M_DEV + 4 * H_DEV) - 1).astype(jnp.int32)
    mesh_receiver = with_ends(jax.random.randint(part_keys[6], (EDGES,), 0, M_DEV), jax.random.fold_in(part_keys[6], 1), 0, M_DEV - 1).astype(jnp.int32)
    halo_rows = with_ends(jax.random.randint(part_keys[7], (HALO,), 0, M_DEV), jax.random.fold_in(part_keys[7], 1), 0, M_DEV - 1).astype(jnp.int32)
    weights = gaussian(splits[8], (13, D, D), D ** -0.5, 0.25, ((1, 2),))
    biases = gaussian(splits[9], (4, D), 0.5, 3.0, (), jnp.float32)
    gains = jnp.clip(1.0 + 0.1 * jax.random.normal(splits[10], (4, D), jnp.float32), 0.5, 1.5)
    return {"grid_latent": grid_latent, "grid_owner": grid_owner, "grid_target": grid_target, "mesh_latent": mesh_latent, "edge_latent": edge_latent, "mesh_sender": mesh_sender, "mesh_receiver": mesh_receiver, "halo_rows": halo_rows, "weights": weights, "biases": biases, "gains": gains}


EPSILON = 1e-05

def layer_norm(values, scale):
    middle = lax.optimization_barrier(jnp.mean(values, axis=-1, keepdims=True))
    spread = lax.optimization_barrier(jnp.mean(jnp.square(values - middle), axis=-1, keepdims=True))
    return (values - middle) * lax.rsqrt(spread + EPSILON) * scale

def reference(grid_latent, grid_owner, grid_target, mesh_latent, edge_latent, mesh_sender, mesh_receiver, halo_rows, weights, biases, gains):
    devices = N_LAT * N_LON * N_CH
    mesh_count = mesh_latent.shape[0]
    mesh_part = jnp.dot(mesh_latent, weights[1], preferred_element_type=jnp.float32)

    def encode(total, index):
        rows = lax.dynamic_slice_in_dim(grid_latent, index * G_DEV, G_DEV, 0)
        owner = lax.dynamic_slice_in_dim(grid_owner, index * G_DEV, G_DEV, 0)[:, 0]
        aims = lax.dynamic_slice_in_dim(grid_target, index * G_DEV, G_DEV, 0)
        target_dev = owner * N_CH + index % N_CH
        nodes = (target_dev * M_DEV)[:, None] + aims
        grid_part = jnp.dot(rows, weights[0], preferred_element_type=jnp.float32)
        pre = grid_part[:, None, :] + mesh_part[nodes] + biases[0]
        hidden = jax.nn.silu(pre).astype(jnp.bfloat16)
        notes = layer_norm(jnp.dot(hidden.reshape(-1, D), weights[2], preferred_element_type=jnp.float32), gains[0])
        return (total.at[nodes.reshape(-1)].add(notes), None)
    encoded, _ = lax.scan(encode, jnp.zeros((mesh_count, D), jnp.float32), jnp.arange(devices, dtype=jnp.int32))
    encoded_sum = encoded.astype(jnp.bfloat16)
    pre = jnp.dot(mesh_latent, weights[3], preferred_element_type=jnp.float32) + jnp.dot(encoded_sum, weights[4], preferred_element_type=jnp.float32) + biases[1]
    node_hidden = jax.nn.silu(pre).astype(jnp.bfloat16)
    mesh_mid = (mesh_latent.astype(jnp.float32) + layer_norm(jnp.dot(node_hidden, weights[5], preferred_element_type=jnp.float32), gains[1])).astype(jnp.bfloat16)
    edge_index = jnp.arange(EDGES, dtype=jnp.int32)
    device = edge_index // E_DEV
    lat_pos = device // (N_LON * N_CH)
    lon_pos = device // N_CH % N_LON
    core = device % N_CH
    offset = jnp.clip(mesh_sender - M_DEV, 0, 4 * H_DEV - 1)
    piece = offset // H_DEV
    entry = offset % H_DEV
    lat_step = jnp.where(piece == 0, -1, jnp.where(piece == 1, 1, 0)).astype(jnp.int32)
    lon_step = jnp.where(piece == 2, -1, jnp.where(piece == 3, 1, 0)).astype(jnp.int32)
    neighbour = ((lat_pos + lat_step) % N_LAT * N_LON + (lon_pos + lon_step) % N_LON) * N_CH + core
    remote = neighbour * M_DEV + halo_rows[neighbour * H_DEV + entry]
    sender_node = jnp.where(mesh_sender < M_DEV, device * M_DEV + mesh_sender, remote).astype(jnp.int32)
    receiver_node = (device * M_DEV + mesh_receiver).astype(jnp.int32)
    sender_part = jnp.dot(mesh_mid, weights[7], preferred_element_type=jnp.float32)
    receiver_part = jnp.dot(mesh_mid, weights[8], preferred_element_type=jnp.float32)

    def process(total, index):
        start = index * E_DEV
        edges = lax.dynamic_slice_in_dim(edge_latent, start, E_DEV, 0)
        senders = lax.dynamic_slice_in_dim(sender_node, start, E_DEV, 0)
        receivers = lax.dynamic_slice_in_dim(receiver_node, start, E_DEV, 0)
        pre = jnp.dot(edges, weights[6], preferred_element_type=jnp.float32) + sender_part[senders] + receiver_part[receivers] + biases[2]
        hidden = jax.nn.silu(pre).astype(jnp.bfloat16)
        notes = layer_norm(jnp.dot(hidden, weights[9], preferred_element_type=jnp.float32), gains[2])
        return (total.at[receivers].add(notes), None)
    processed, _ = lax.scan(process, jnp.zeros((mesh_count, D), jnp.float32), jnp.arange(devices, dtype=jnp.int32))
    processed_sum = processed.astype(jnp.bfloat16)
    pre = jnp.dot(mesh_mid, weights[10], preferred_element_type=jnp.float32) + jnp.dot(processed_sum, weights[11], preferred_element_type=jnp.float32) + biases[3]
    update_hidden = jax.nn.silu(pre).astype(jnp.bfloat16)
    return (mesh_mid.astype(jnp.float32) + layer_norm(jnp.dot(update_hidden, weights[12], preferred_element_type=jnp.float32), gains[3])).astype(jnp.bfloat16)
```

```python
import functools

import jax
import jax.numpy as jnp
from jax import lax
from jax.experimental import pallas as pl
from jax.experimental.pallas import tpu as pltpu
from jax.sharding import PartitionSpec as P

EPSILON = 1e-05
LANES = 128
AIM_ROWS = 16
F32 = jnp.float32
BF16 = jnp.bfloat16
ANY = pl.BlockSpec(memory_space=pl.ANY)
VMEM = pl.BlockSpec(memory_space=pltpu.VMEM)
VMEM_LIMIT = 24 * 1024 * 1024


def mm(left, right):
    return jnp.dot(left, right, preferred_element_type=F32)


def mm_nt(left, right):
    return lax.dot_general(left, right, (((1,), (1,)), ((), ())), preferred_element_type=F32)


def silu(values):
    half = 0.5 * values
    return (half + half * jnp.tanh(half)).astype(BF16)


def normed(values):
    middle = jnp.mean(values, axis=-1, keepdims=True)
    centred = values - middle
    spread = jnp.mean(centred * centred, axis=-1, keepdims=True)
    return centred * lax.rsqrt(spread + EPSILON)


def as_bf16(mask):
    return jnp.where(mask, 1.0, 0.0).astype(BF16)


def down(row, count):
    return as_bf16(lax.broadcasted_iota(jnp.int32, (count, row.shape[1]), 0) == row)


def along(column, count):
    return as_bf16(lax.broadcasted_iota(jnp.int32, (column.shape[0], count), 1) == column)


def turned(row):
    wide = jnp.broadcast_to(row.astype(F32), (8, row.shape[1]))
    return jnp.transpose(wide)[:, :1].astype(jnp.int32)


def fetch(mine_ref, other_ref, into, sems, picks):
    half = mine_ref.shape[1]
    core = lax.axis_index("ch")
    copies = []
    for i, (pick, place) in enumerate(picks):
        for j, (ref, at) in enumerate(((mine_ref, core), (other_ref, 1 - core))):
            rows = pl.ds(pl.multiple_of(at * half, half), half)
            copy = pltpu.make_async_copy(
                ref.at[pick], into[place].at[rows, :], sems.at[2 * i + j]
            )
            copy.start()
            copies.append(copy)
    return copies


def arrive(copies, count=1):
    for copy in copies[: 2 * count]:
        copy.wait()
    del copies[: 2 * count]


def dispatch_kernel(owners, capacity, exchange, owner_ref, target_ref, latent_ref, *outs):
    rows, width = latent_ref.shape
    padded = max(16, owners)
    number = lax.broadcasted_iota(jnp.int32, (padded, rows), 0)
    named = number == owner_ref[...]
    before = as_bf16(
        lax.broadcasted_iota(jnp.int32, (rows, rows), 0)
        < lax.broadcasted_iota(jnp.int32, (rows, rows), 1)
    )
    rank = mm(as_bf16(named), before).astype(jnp.int32)
    place = jnp.sum(jnp.where(named, number * capacity + rank, 0), axis=0, keepdims=True)
    aims = jnp.concatenate(
        [
            (target_ref[...] + 1).astype(F32),
            jnp.zeros((AIM_ROWS - target_ref.shape[0], rows), F32),
        ],
        axis=0,
    ).astype(BF16)
    latent = latent_ref[...]
    me = lax.axis_index("lat") * lax.axis_size("lon") + lax.axis_index("lon")
    for q, out in enumerate(outs):
        base = (me ^ q) * capacity if exchange else q * LANES
        pick = as_bf16(lax.broadcasted_iota(jnp.int32, (LANES, rows), 0) + base == place)
        data = mm(pick, latent).astype(BF16)
        for j in range(width // LANES):
            out[j * LANES : (j + 1) * LANES, :] = data[:, j * LANES : (j + 1) * LANES]
        out[width : width + AIM_ROWS, :] = mm_nt(aims, pick).astype(BF16)


def encode(chunks, first, third, mesh_part, bias):
    width = first.shape[0]
    nodes = mesh_part.shape[0]
    total = None
    for chunk in chunks:
        rows = jnp.concatenate(
            [chunk[j * LANES : (j + 1) * LANES, :] for j in range(width // LANES)], axis=1
        )
        aims = chunk[width : width + AIM_ROWS, :].astype(F32)
        columns = jnp.transpose(aims).astype(jnp.int32) - 1
        lines = aims.astype(jnp.int32) - 1
        part = mm(rows, first) + bias
        hidden = jnp.concatenate(
            [silu(part + mm(along(columns[:, k : k + 1], nodes), mesh_part)) for k in range(2)],
            axis=0,
        )
        notes = normed(mm(hidden, third)).astype(BF16)
        spread = jnp.concatenate([down(lines[k : k + 1, :], nodes) for k in range(2)], axis=1)
        partial = mm(spread, notes)
        total = partial if total is None else total + partial
    return total


def first_kernel(mine, other, mesh, chunk, biases, sum_out, part_out, first_out, third_out, second, sems):
    into = [first_out, second, third_out]
    copies = fetch(mine, other, into, sems, [(1, 1), (0, 0), (2, 2)])
    arrive(copies)
    part = mm(mesh[...], second[...]).astype(BF16)
    part_out[...] = part
    arrive(copies, 2)
    sum_out[...] = encode([chunk], first_out[...], third_out[...], part, biases[0:1, :])


def more_kernel(total, part, first, third, biases, *rest):
    *chunks, out = rest
    out[...] = total[...] + encode(chunks, first[...], third[...], part[...], biases[0:1, :])


def node_kernel(total, part, first, third, biases, gains, mine, other, mesh, lend, *rest):
    *chunks, mid_out, lent_out, node_maps, sems = rest
    maps = [node_maps.at[0], node_maps.at[1], node_maps.at[2]]
    copies = fetch(mine, other, maps, sems, [(3, 0), (4, 1), (5, 2)])
    sums = total[...] + encode(chunks, first[...], third[...], part[...], biases[0:1, :])
    encoded = (sums * gains[0:1, :]).astype(BF16)
    arrive(copies, 3)
    latent = mesh[...]
    hidden = silu(mm(latent, node_maps[0]) + mm(encoded, node_maps[1]) + biases[1:2, :])
    mid = (
        latent.astype(F32) + normed(mm(hidden, node_maps[2])) * gains[1:2, :]
    ).astype(BF16)
    mid_out[...] = mid
    picks = along(turned(lend[...]), mid.shape[0])
    lent_out[...] = mm(picks, mid).astype(BF16)


def local_kernel(mid_ref, edges, sender, receiver, biases, mine, other, pre_out, maps, sems):
    into = [maps.at[0], maps.at[1], maps.at[2]]
    copies = fetch(mine, other, into, sems, [(6, 0), (7, 1), (8, 2)])
    mid = mid_ref[...]
    nodes = mid.shape[0]
    at_sender = along(turned(sender[...]), nodes)
    at_receiver = along(turned(receiver[...]), nodes)
    arrive(copies, 3)
    pre = mm(edges[...], maps[0]) + biases[2:3, :]
    pre = pre + mm(at_sender, mm(mid, maps[1]).astype(BF16))
    pre_out[...] = pre + mm(at_receiver, mm(mid, maps[2]).astype(BF16))


def process_kernel(pre, mid_ref, sender, receiver, biases, gains, mine, other, *rest):
    *lent, out, maps, sems = rest
    into = [maps.at[i] for i in range(5)]
    copies = fetch(
        mine, other, into, sems, [(7, 0), (9, 1), (10, 2), (11, 3), (12, 4)]
    )
    mid = mid_ref[...]
    nodes = mid.shape[0]
    table = jnp.concatenate([ref[...] for ref in lent], axis=0)
    depth = lent[0].shape[0]
    entry = sender[...] - nodes
    if len(lent) == 3:
        entry = jnp.where(entry >= 3 * depth, entry - depth, entry)
    from_halo = along(turned(entry), len(lent) * depth)
    arrive(copies)
    halo = mm(table, maps[0]).astype(BF16)
    hidden = silu(pre[...] + mm(from_halo, halo))
    arrive(copies)
    notes = normed(mm(hidden, maps[1])).astype(BF16)
    sums = mm(down(receiver[...], nodes), notes)
    processed = (sums * gains[2:3, :]).astype(BF16)
    arrive(copies, 3)
    hidden = silu(mm(mid, maps[2]) + mm(processed, maps[3]) + biases[3:4, :])
    out[...] = (
        mid.astype(F32) + normed(mm(hidden, maps[4])) * gains[3:4, :]
    ).astype(BF16)


def call(kernel, outs, ins, specs, scratch=(), flops=0, moved=0):
    return pl.pallas_call(
        kernel,
        out_shape=[jax.ShapeDtypeStruct(shape, kind) for shape, kind in outs],
        in_specs=specs,
        out_specs=[VMEM] * len(outs),
        scratch_shapes=list(scratch),
        compiler_params=pltpu.CompilerParams(vmem_limit_bytes=VMEM_LIMIT),
        cost_estimate=pl.CostEstimate(flops=flops, bytes_accessed=moved, transcendentals=0),
    )(*ins)


def swap(value, axes, step):
    count = lax.axis_size(axes)
    return lax.ppermute(value, axes, [(i, i ^ step) for i in range(count)])


def shift(value, axis, step):
    count = lax.axis_size(axis)
    return lax.ppermute(value, axis, [(i, (i + step) % count) for i in range(count)])


def sent_whole(chunks, owners, capacity, width):
    count = len(chunks)
    stack = jnp.stack(chunks)
    rows = stack[:, :width].reshape(count, width // LANES, LANES, LANES)
    rows = rows.transpose(0, 2, 1, 3).reshape(owners, capacity, width)
    aims = stack[:, width:].transpose(0, 2, 1).reshape(owners, capacity, AIM_ROWS)
    rows, aims = (
        lax.all_to_all(part, ("lat", "lon"), split_axis=0, concat_axis=0, tiled=True)
        for part in (rows, aims)
    )
    rows = rows.reshape(count, LANES, width // LANES, LANES).transpose(0, 2, 1, 3)
    aims = aims.reshape(count, LANES, AIM_ROWS).transpose(0, 2, 1)
    stack = jnp.concatenate([rows.reshape(count, width, LANES), aims], axis=1)
    return [stack[i] for i in range(count)]


def per_device(
    grid_latent,
    grid_owner,
    grid_target,
    mesh_latent,
    edge_latent,
    mesh_sender,
    mesh_receiver,
    halo_rows,
    weights,
    biases,
    gains,
):
    rows_dev, width = grid_latent.shape
    nodes = mesh_latent.shape[0]
    edges = edge_latent.shape[0]
    lon_count = lax.axis_size("lon")
    owners = lax.axis_size("lat") * lon_count
    capacity = max(2, 2 * rows_dev // owners)
    exchange = capacity == LANES and owners <= 16 and owners & (owners - 1) == 0
    square = (width, width)

    other = swap(weights, "ch", 1)

    count = owners * capacity // LANES
    chunk_shape = ((width + AIM_ROWS, LANES), BF16)
    chunks = call(
        functools.partial(dispatch_kernel, owners, capacity, exchange),
        [chunk_shape] * count,
        (grid_owner.T, grid_target.T, grid_latent),
        [VMEM] * 3,
        flops=10**9,
        moved=2 * 10**6,
    )
    if exchange:
        arrived = {0: chunks[0]}
        for step in [4, 5, 6, 7, 2, 3, 1] if owners == 8 else range(1, owners):
            arrived[step] = swap(chunks[step], ("lat", "lon"), step)
        groups = [[0], [4, 5], [6, 7, 2], [3, 1]] if owners == 8 else [[0], list(range(1, owners))]
    else:
        arrived = dict(enumerate(sent_whole(chunks, owners, capacity, width)))
        groups = [[0], list(range(1, count))]

    sems = lambda n: pltpu.SemaphoreType.DMA((2 * n,))
    total, part, first, third = call(
        first_kernel,
        [((nodes, width), F32), ((nodes, width), BF16), (square, BF16), (square, BF16)],
        (weights, other, mesh_latent, arrived[0], biases),
        [ANY, ANY, VMEM, VMEM, VMEM],
        [pltpu.VMEM(square, BF16), sems(3)],
        flops=5 * 10**8,
        moved=3 * 10**6,
    )
    for group in groups[1:-1]:
        (total,) = call(
            more_kernel,
            [((nodes, width), F32)],
            (total, part, first, third, biases, *[arrived[i] for i in group]),
            [VMEM] * (5 + len(group)),
            flops=4 * 10**8 * len(group),
            moved=2 * 10**6,
        )
    mid, lent = call(
        node_kernel,
        [((nodes, width), BF16), ((halo_rows.shape[0], width), BF16)],
        (total, part, first, third, biases, gains, weights, other, mesh_latent)
        + (halo_rows.reshape(1, -1), *[arrived[i] for i in groups[-1]]),
        [VMEM] * 6 + [ANY, ANY, VMEM, VMEM] + [VMEM] * len(groups[-1]),
        [pltpu.VMEM((3, *square), BF16), sems(3)],
        flops=10**9,
        moved=3 * 10**6,
    )
    halo = [shift(lent, "lat", 1), shift(lent, "lat", -1), shift(lent, "lon", 1)]
    if lon_count != 2:
        halo.append(shift(lent, "lon", -1))
    sender, receiver = mesh_sender.reshape(1, -1), mesh_receiver.reshape(1, -1)
    (pre,) = call(
        local_kernel,
        [((edges, width), F32)],
        (mid, edge_latent, sender, receiver, biases, weights, other),
        [VMEM] * 5 + [ANY, ANY],
        [pltpu.VMEM((3, *square), BF16), sems(3)],
        flops=10**9,
        moved=3 * 10**6,
    )
    (out,) = call(
        process_kernel,
        [((nodes, width), BF16)],
        (pre, mid, sender, receiver, biases, gains, weights, other, *halo),
        [VMEM] * 6 + [ANY, ANY] + [VMEM] * len(halo),
        [pltpu.VMEM((5, *square), BF16), sems(5)],
        flops=10**9,
        moved=3 * 10**6,
    )
    return out


def solution(mesh):
    in_specs = (
        P(("member", "lat", "lon", "ch"), None),
        P(("member", "lat", "lon", "ch"), None),
        P(("member", "lat", "lon", "ch"), None),
        P(("member", "lat", "lon", "ch"), None),
        P(("member", "lat", "lon", "ch"), None),
        P(("member", "lat", "lon", "ch")),
        P(("member", "lat", "lon", "ch")),
        P(("member", "lat", "lon", "ch")),
        P(None, "ch", None),
        P(),
        P(),
    )
    out_specs = P(("member", "lat", "lon", "ch"), None)
    return jax.shard_map(
        per_device, mesh=mesh, in_specs=in_specs, out_specs=out_specs, check_vma=False
    )
```

```python
import functools

import jax
import jax.numpy as jnp
from jax import lax
from jax.experimental import pallas as pl
from jax.experimental.pallas import tpu as pltpu
from jax.sharding import PartitionSpec as P

EPSILON = 1e-05
LANES = 128
AIM_ROWS = 16
F32 = jnp.float32
BF16 = jnp.bfloat16
HBM = pl.BlockSpec(memory_space=pltpu.HBM)
VMEM = pl.BlockSpec(memory_space=pltpu.VMEM)
VMEM_LIMIT = 24 * 1024 * 1024


def mm(left, right):
    return jnp.dot(left, right, preferred_element_type=F32)


def mm_nt(left, right):
    return lax.dot_general(left, right, (((1,), (1,)), ((), ())), preferred_element_type=F32)


def silu(values):
    half = 0.5 * values
    return (half + half * jnp.tanh(half)).astype(BF16)


def normed(values):
    middle = jnp.mean(values, axis=-1, keepdims=True)
    centred = values - middle
    spread = jnp.mean(centred * centred, axis=-1, keepdims=True)
    return centred * lax.rsqrt(spread + EPSILON)


def as_bf16(mask):
    return jnp.where(mask, 1.0, 0.0).astype(BF16)


def down(row, count):
    return as_bf16(lax.broadcasted_iota(jnp.int32, (count, row.shape[1]), 0) == row)


def along(column, count):
    return as_bf16(lax.broadcasted_iota(jnp.int32, (column.shape[0], count), 1) == column)


def turned(row):
    wide = jnp.broadcast_to(row.astype(F32), (8, row.shape[1]))
    return jnp.transpose(wide)[:, :1].astype(jnp.int32)


def halves(rows):
    half = rows.shape[1] // 2
    low, high = rows[:, :half], rows[:, half:]
    first = lax.axis_index("ch") == 0
    return jnp.where(first, low, high), jnp.where(first, high, low)


def through(rows, maps, pick):
    here, there = halves(rows)
    return mm(here, maps[0][pick]) + mm(there, maps[1][pick])


def dispatch_kernel(owners, capacity, exchange, owner_in, target_in, latent_in, *rest):
    *outs, owner_ref, target_ref, latent_ref, sems = rest
    rows, width = latent_ref.shape
    pairs = ((owner_in, owner_ref), (target_in, target_ref), (latent_in, latent_ref))
    copies = [pltpu.make_async_copy(*pair, sems.at[i]) for i, pair in enumerate(pairs)]
    for copy in copies:
        copy.start()
    padded = max(16, owners)
    number = lax.broadcasted_iota(jnp.int32, (padded, rows), 0)
    before = as_bf16(
        lax.broadcasted_iota(jnp.int32, (rows, rows), 0)
        < lax.broadcasted_iota(jnp.int32, (rows, rows), 1)
    )
    copies[0].wait()
    named = number == owner_ref[...]
    rank = mm(as_bf16(named), before).astype(jnp.int32)
    place = jnp.sum(jnp.where(named, number * capacity + rank, 0), axis=0, keepdims=True)
    copies[1].wait()
    aims = jnp.concatenate(
        [
            (target_ref[...] + 1).astype(F32),
            jnp.zeros((AIM_ROWS - target_ref.shape[0], rows), F32),
        ],
        axis=0,
    ).astype(BF16)
    copies[2].wait()
    latent = latent_ref[...]
    me = lax.axis_index("lat") * lax.axis_size("lon") + lax.axis_index("lon")
    for q, out in enumerate(outs):
        base = (me ^ q) * capacity if exchange else q * LANES
        pick = as_bf16(lax.broadcasted_iota(jnp.int32, (LANES, rows), 0) + base == place)
        data = mm(pick, latent).astype(BF16)
        for j in range(width // LANES):
            out[j * LANES : (j + 1) * LANES, :] = data[:, j * LANES : (j + 1) * LANES]
        out[width : width + AIM_ROWS, :] = mm_nt(aims, pick).astype(BF16)


def encode(chunks, maps, mesh_part, bias):
    nodes, width = mesh_part.shape
    total = None
    for chunk in chunks:
        rows = jnp.concatenate(
            [chunk[j * LANES : (j + 1) * LANES, :] for j in range(width // LANES)], axis=1
        )
        aims = chunk[width : width + AIM_ROWS, :].astype(F32)
        columns = jnp.transpose(aims).astype(jnp.int32) - 1
        lines = aims.astype(jnp.int32) - 1
        part = through(rows, maps, 0) + bias
        hidden = jnp.concatenate(
            [silu(part + mm(along(columns[:, k : k + 1], nodes), mesh_part)) for k in range(2)],
            axis=0,
        )
        notes = normed(through(hidden, maps, 2)).astype(BF16)
        spread = jnp.concatenate([down(lines[k : k + 1, :], nodes) for k in range(2)], axis=1)
        partial = mm(spread, notes)
        total = partial if total is None else total + partial
    return total


def first_kernel(mine, other, mesh, chunk, biases, sum_out, part_out):
    maps = (mine, other)
    part = through(mesh[...], maps, 1).astype(BF16)
    part_out[...] = part
    sum_out[...] = encode([chunk], maps, part, biases[0:1, :])


def more_kernel(total, part, mine, other, biases, *rest):
    *chunks, out = rest
    out[...] = total[...] + encode(chunks, (mine, other), part[...], biases[0:1, :])


def node_kernel(total, part, mine, other, biases, gains, mesh, lend, *rest):
    *chunks, mid_out, lent_out = rest
    maps = (mine, other)
    sums = total[...] + encode(chunks, maps, part[...], biases[0:1, :])
    encoded = (sums * gains[0:1, :]).astype(BF16)
    latent = mesh[...]
    hidden = silu(through(latent, maps, 3) + through(encoded, maps, 4) + biases[1:2, :])
    mid = (
        latent.astype(F32) + normed(through(hidden, maps, 5)) * gains[1:2, :]
    ).astype(BF16)
    mid_out[...] = mid
    picks = along(turned(lend[...]), mid.shape[0])
    lent_out[...] = mm(picks, mid).astype(BF16)


def local_kernel(mid_ref, edges, sender, receiver, biases, mine, other, pre_out):
    maps = (mine, other)
    mid = mid_ref[...]
    nodes = mid.shape[0]
    at_sender = along(turned(sender[...]), nodes)
    at_receiver = along(turned(receiver[...]), nodes)
    pre = through(edges[...], maps, 6) + biases[2:3, :]
    pre = pre + mm(at_sender, through(mid, maps, 7).astype(BF16))
    pre_out[...] = pre + mm(at_receiver, through(mid, maps, 8).astype(BF16))


def process_kernel(pre, mid_ref, sender, receiver, biases, gains, mine, other, *rest):
    *lent, out = rest
    maps = (mine, other)
    mid = mid_ref[...]
    nodes = mid.shape[0]
    table = jnp.concatenate([ref[...] for ref in lent], axis=0)
    depth = lent[0].shape[0]
    entry = sender[...] - nodes
    if len(lent) == 3:
        entry = jnp.where(entry >= 3 * depth, entry - depth, entry)
    from_halo = along(turned(entry), len(lent) * depth)
    hidden = silu(pre[...] + mm(from_halo, through(table, maps, 7).astype(BF16)))
    notes = normed(through(hidden, maps, 9)).astype(BF16)
    sums = mm(down(receiver[...], nodes), notes)
    processed = (sums * gains[2:3, :]).astype(BF16)
    hidden = silu(through(mid, maps, 10) + through(processed, maps, 11) + biases[3:4, :])
    out[...] = (
        mid.astype(F32) + normed(through(hidden, maps, 12)) * gains[3:4, :]
    ).astype(BF16)


def call(kernel, outs, ins, specs, scratch=(), flops=0, moved=0):
    return pl.pallas_call(
        kernel,
        out_shape=[jax.ShapeDtypeStruct(shape, kind) for shape, kind in outs],
        in_specs=specs,
        out_specs=[VMEM] * len(outs),
        scratch_shapes=list(scratch),
        compiler_params=pltpu.CompilerParams(vmem_limit_bytes=VMEM_LIMIT),
        cost_estimate=pl.CostEstimate(flops=flops, bytes_accessed=moved, transcendentals=0),
    )(*ins)


def swap(value, axes, step):
    count = lax.axis_size(axes)
    return lax.ppermute(value, axes, [(i, i ^ step) for i in range(count)])


def shift(value, axis, step):
    count = lax.axis_size(axis)
    return lax.ppermute(value, axis, [(i, (i + step) % count) for i in range(count)])


def sent_whole(chunks, owners, capacity, width):
    count = len(chunks)
    stack = jnp.stack(chunks)
    rows = stack[:, :width].reshape(count, width // LANES, LANES, LANES)
    rows = rows.transpose(0, 2, 1, 3).reshape(owners, capacity, width)
    aims = stack[:, width:].transpose(0, 2, 1).reshape(owners, capacity, AIM_ROWS)
    rows, aims = (
        lax.all_to_all(part, ("lat", "lon"), split_axis=0, concat_axis=0, tiled=True)
        for part in (rows, aims)
    )
    rows = rows.reshape(count, LANES, width // LANES, LANES).transpose(0, 2, 1, 3)
    aims = aims.reshape(count, LANES, AIM_ROWS).transpose(0, 2, 1)
    stack = jnp.concatenate([rows.reshape(count, width, LANES), aims], axis=1)
    return [stack[i] for i in range(count)]


def per_device(
    grid_latent,
    grid_owner,
    grid_target,
    mesh_latent,
    edge_latent,
    mesh_sender,
    mesh_receiver,
    halo_rows,
    weights,
    biases,
    gains,
):
    rows_dev, width = grid_latent.shape
    nodes = mesh_latent.shape[0]
    edges = edge_latent.shape[0]
    lon_count = lax.axis_size("lon")
    owners = lax.axis_size("lat") * lon_count
    capacity = max(2, 2 * rows_dev // owners)
    exchange = capacity == LANES and owners <= 16 and owners & (owners - 1) == 0

    other = swap(weights, "ch", 1)

    count = owners * capacity // LANES
    chunk_shape = ((width + AIM_ROWS, LANES), BF16)
    chunks = call(
        functools.partial(dispatch_kernel, owners, capacity, exchange),
        [chunk_shape] * count,
        [
            pltpu.with_memory_space_constraint(value, pltpu.HBM)
            for value in (grid_owner.T, grid_target.T, grid_latent)
        ],
        [HBM] * 3,
        [
            pltpu.VMEM((1, rows_dev), jnp.int32),
            pltpu.VMEM((2, rows_dev), jnp.int32),
            pltpu.VMEM((rows_dev, width), BF16),
            pltpu.SemaphoreType.DMA((3,)),
        ],
        flops=10**9,
        moved=2 * 10**6,
    )
    if exchange:
        arrived = {0: chunks[0]}
        for step in [1, 4, 5, 6, 7, 2, 3] if owners == 8 else range(1, owners):
            arrived[step] = swap(chunks[step], ("lat", "lon"), step)
        groups = [[0], [1, 2], [4, 3, 5], [6, 7]] if owners == 8 else [[0], list(range(1, owners))]
    else:
        arrived = dict(enumerate(sent_whole(chunks, owners, capacity, width)))
        groups = [[0], list(range(1, count))]

    total, part = call(
        first_kernel,
        [((nodes, width), F32), ((nodes, width), BF16)],
        (weights, other, mesh_latent, arrived[0], biases),
        [VMEM] * 5,
        flops=5 * 10**8,
        moved=3 * 10**6,
    )
    for group in groups[1:-1]:
        (total,) = call(
            more_kernel,
            [((nodes, width), F32)],
            (total, part, weights, other, biases, *[arrived[i] for i in group]),
            [VMEM] * (5 + len(group)),
            flops=4 * 10**8 * len(group),
            moved=2 * 10**6,
        )
    mid, lent = call(
        node_kernel,
        [((nodes, width), BF16), ((halo_rows.shape[0], width), BF16)],
        (total, part, weights, other, biases, gains, mesh_latent)
        + (halo_rows.reshape(1, -1), *[arrived[i] for i in groups[-1]]),
        [VMEM] * (8 + len(groups[-1])),
        flops=10**9,
        moved=3 * 10**6,
    )
    halo = [shift(lent, "lat", 1), shift(lent, "lat", -1), shift(lent, "lon", 1)]
    if lon_count != 2:
        halo.append(shift(lent, "lon", -1))
    sender, receiver = mesh_sender.reshape(1, -1), mesh_receiver.reshape(1, -1)
    (pre,) = call(
        local_kernel,
        [((edges, width), F32)],
        (mid, edge_latent, sender, receiver, biases, weights, other),
        [VMEM] * 7,
        flops=10**9,
        moved=3 * 10**6,
    )
    (out,) = call(
        process_kernel,
        [((nodes, width), BF16)],
        (pre, mid, sender, receiver, biases, gains, weights, other, *halo),
        [VMEM] * (8 + len(halo)),
        flops=10**9,
        moved=3 * 10**6,
    )
    return out


def solution(mesh):
    in_specs = (
        P(("member", "lat", "lon", "ch"), None),
        P(("member", "lat", "lon", "ch"), None),
        P(("member", "lat", "lon", "ch"), None),
        P(("member", "lat", "lon", "ch"), None),
        P(("member", "lat", "lon", "ch"), None),
        P(("member", "lat", "lon", "ch")),
        P(("member", "lat", "lon", "ch")),
        P(("member", "lat", "lon", "ch")),
        P(None, "ch", None),
        P(),
        P(),
    )
    out_specs = P(("member", "lat", "lon", "ch"), None)
    return jax.shard_map(
        per_device, mesh=mesh, in_specs=in_specs, out_specs=out_specs, check_vma=False
    )
```

```python
import functools

import jax
import jax.numpy as jnp
from jax import lax
from jax.experimental import pallas as pl
from jax.experimental.pallas import tpu as pltpu
from jax.sharding import PartitionSpec as P

EPSILON = 1e-05
LANES = 128
AIM_ROWS = 16
F32 = jnp.float32
BF16 = jnp.bfloat16
HBM = pl.BlockSpec(memory_space=pltpu.HBM)
VMEM = pl.BlockSpec(memory_space=pltpu.VMEM)
VMEM_LIMIT = 24 * 1024 * 1024


def mm(left, right):
    return jnp.dot(left, right, preferred_element_type=F32)


def mm_nt(left, right):
    return lax.dot_general(left, right, (((1,), (1,)), ((), ())), preferred_element_type=F32)


def silu(values):
    half = 0.5 * values
    return (half + half * jnp.tanh(half)).astype(BF16)


def normed(values):
    middle = jnp.mean(values, axis=-1, keepdims=True)
    centred = values - middle
    spread = jnp.mean(centred * centred, axis=-1, keepdims=True)
    return centred * lax.rsqrt(spread + EPSILON)


def as_bf16(mask):
    return jnp.where(mask, 1.0, 0.0).astype(BF16)


def down(row, count):
    return as_bf16(lax.broadcasted_iota(jnp.int32, (count, row.shape[1]), 0) == row)


def along(column, count):
    return as_bf16(lax.broadcasted_iota(jnp.int32, (column.shape[0], count), 1) == column)


def turned(row):
    wide = jnp.broadcast_to(row.astype(F32), (8, row.shape[1]))
    return jnp.transpose(wide)[:, :1].astype(jnp.int32)


def halves(rows):
    half = rows.shape[1] // 2
    low, high = rows[:, :half], rows[:, half:]
    first = lax.axis_index("ch") == 0
    return jnp.where(first, low, high), jnp.where(first, high, low)


def through(rows, maps, pick):
    here, there = halves(rows)
    return mm(here, maps[0][pick]) + mm(there, maps[1][pick])


def packed(place, aims, latent, base, out):
    rows, width = latent.shape
    pick = as_bf16(lax.broadcasted_iota(jnp.int32, (LANES, rows), 0) + base == place)
    data = mm(pick, latent).astype(BF16)
    for j in range(width // LANES):
        out[j * LANES : (j + 1) * LANES, :] = data[:, j * LANES : (j + 1) * LANES]
    out[width : width + AIM_ROWS, :] = mm_nt(aims, pick).astype(BF16)


def base_of(step, capacity, exchange):
    if not exchange:
        return step * LANES
    lats, lons = lax.axis_size("lat"), lax.axis_size("lon")
    lat, lon = lax.axis_index("lat"), lax.axis_index("lon")
    owner = lax.rem(lat + step // lons, lats) * lons + lax.rem(lon + step % lons, lons)
    return owner * capacity


def place_kernel(owners, capacity, exchange, step, owner_in, target_in, latent_in, *rest):
    out, place_out, aims_out, owner_ref, target_ref, latent_ref, sems = rest
    rows, width = latent_ref.shape
    pairs = ((owner_in, owner_ref), (target_in, target_ref), (latent_in, latent_ref))
    copies = [pltpu.make_async_copy(*pair, sems.at[i]) for i, pair in enumerate(pairs)]
    for copy in copies:
        copy.start()
    number = lax.broadcasted_iota(jnp.int32, (max(16, owners), rows), 0)
    before = as_bf16(
        lax.broadcasted_iota(jnp.int32, (rows, rows), 0)
        < lax.broadcasted_iota(jnp.int32, (rows, rows), 1)
    )
    copies[0].wait()
    named = number == owner_ref[...]
    rank = mm(as_bf16(named), before).astype(jnp.int32)
    place = jnp.sum(jnp.where(named, number * capacity + rank, 0), axis=0, keepdims=True)
    copies[1].wait()
    aims = jnp.concatenate(
        [
            (target_ref[...] + 1).astype(F32),
            jnp.zeros((AIM_ROWS - target_ref.shape[0], rows), F32),
        ],
        axis=0,
    ).astype(BF16)
    place_out[...] = place
    aims_out[...] = aims
    copies[2].wait()
    packed(place, aims, latent_ref[...], base_of(step, capacity, exchange), out)


def dispatch_kernel(capacity, exchange, steps, place_ref, aims_ref, latent_ref, *outs):
    place, aims, latent = place_ref[...], aims_ref[...], latent_ref[...]
    for step, out in zip(steps, outs):
        packed(place, aims, latent, base_of(step, capacity, exchange), out)


def encode(chunks, maps, mesh_part, bias):
    nodes, width = mesh_part.shape
    rows = jnp.concatenate(
        [
            jnp.concatenate(
                [chunk[j * LANES : (j + 1) * LANES, :] for j in range(width // LANES)], axis=1
            )
            for chunk in chunks
        ],
        axis=0,
    )
    lines = [chunk[width : width + AIM_ROWS, :].astype(F32) for chunk in chunks]
    columns = [jnp.transpose(line).astype(jnp.int32) - 1 for line in lines]
    lines = [line.astype(jnp.int32) - 1 for line in lines]
    part = through(rows, maps, 0) + bias
    picks = jnp.concatenate(
        [along(column[:, k : k + 1], nodes) for k in range(2) for column in columns], axis=0
    )
    spread = jnp.concatenate(
        [down(line[k : k + 1, :], nodes) for k in range(2) for line in lines], axis=1
    )
    hidden = silu(jnp.concatenate([part, part], axis=0) + mm(picks, mesh_part))
    return mm(spread, normed(through(hidden, maps, 2)).astype(BF16))


def first_kernel(mine, other, mesh, chunk, biases, sum_out, part_out, ahead_out):
    maps = (mine, other)
    latent = mesh[...]
    part = through(latent, maps, 1).astype(BF16)
    part_out[...] = part
    ahead_out[...] = through(latent, maps, 3) + biases[1:2, :]
    sum_out[...] = encode([chunk], maps, part, biases[0:1, :])


def more_kernel(total, part, mine, other, biases, *rest):
    *chunks, out = rest
    out[...] = total[...] + encode(chunks, (mine, other), part[...], biases[0:1, :])


def node_kernel(total, part, ahead, mine, other, biases, gains, mesh, lend, *rest):
    *chunks, mid_out, lent_out = rest
    maps = (mine, other)
    sums = total[...] + encode(chunks, maps, part[...], biases[0:1, :])
    encoded = (sums * gains[0:1, :]).astype(BF16)
    hidden = silu(ahead[...] + through(encoded, maps, 4))
    mid = (
        mesh[...].astype(F32) + normed(through(hidden, maps, 5)) * gains[1:2, :]
    ).astype(BF16)
    mid_out[...] = mid
    picks = along(turned(lend[...]), mid.shape[0])
    lent_out[...] = mm(picks, mid).astype(BF16)


def local_kernel(pieces, depth, mid_ref, edges, sender, receiver, biases, mine, other, *outs):
    pre_out, ahead_out, picks_out, spread_out = outs
    maps = (mine, other)
    mid = mid_ref[...]
    nodes = mid.shape[0]
    number = sender[...]
    entry = number - nodes
    if pieces == 3:
        entry = jnp.where(entry >= 3 * depth, entry - depth, entry)
    odd = lax.rem(lax.axis_index("lat"), 2) == 1
    crossed = jnp.where(entry < depth, entry + depth, jnp.where(entry < 2 * depth, entry - depth, entry))
    entry = jnp.where(odd & (entry >= 0), crossed, entry)
    picks_out[...] = along(turned(entry), pieces * depth)
    spread_out[...] = down(receiver[...], nodes)
    at_sender = along(turned(number), nodes)
    at_receiver = along(turned(receiver[...]), nodes)
    ahead_out[...] = through(mid, maps, 10) + biases[3:4, :]
    pre = through(edges[...], maps, 6) + biases[2:3, :]
    pre = pre + mm(at_sender, through(mid, maps, 7).astype(BF16))
    pre_out[...] = pre + mm(at_receiver, through(mid, maps, 8).astype(BF16))


def process_kernel(pre, ahead, picks, spread, mid, gains, mine, other, *rest):
    *lent, out = rest
    maps = (mine, other)
    table = jnp.concatenate([ref[...] for ref in lent], axis=0)
    hidden = silu(pre[...] + mm(picks[...], through(table, maps, 7).astype(BF16)))
    notes = normed(through(hidden, maps, 9)).astype(BF16)
    processed = (mm(spread[...], notes) * gains[2:3, :]).astype(BF16)
    hidden = silu(ahead[...] + through(processed, maps, 11))
    out[...] = (
        mid[...].astype(F32) + normed(through(hidden, maps, 12)) * gains[3:4, :]
    ).astype(BF16)


def call(kernel, outs, ins, specs, scratch=(), flops=0, moved=0):
    return pl.pallas_call(
        kernel,
        out_shape=[jax.ShapeDtypeStruct(shape, kind) for shape, kind in outs],
        in_specs=specs,
        out_specs=[VMEM] * len(outs),
        scratch_shapes=list(scratch),
        compiler_params=pltpu.CompilerParams(vmem_limit_bytes=VMEM_LIMIT),
        cost_estimate=pl.CostEstimate(flops=flops, bytes_accessed=moved, transcendentals=0),
    )(*ins)


def swap(value, axes, step):
    count = lax.axis_size(axes)
    return lax.ppermute(value, axes, [(i, i ^ step) for i in range(count)])


def moved(value, step):
    lats, lons = lax.axis_size("lat"), lax.axis_size("lon")
    pairs = []
    for i in range(lats * lons):
        lat, lon = (i // lons + step // lons) % lats, (i % lons + step % lons) % lons
        pairs.append((i, lat * lons + lon))
    return lax.ppermute(value, ("lat", "lon"), pairs)


def shift(value, axis, step):
    count = lax.axis_size(axis)
    return lax.ppermute(value, axis, [(i, (i + step) % count) for i in range(count)])


def paired(value, axis, first):
    count = lax.axis_size(axis)
    pairs = []
    for i in range(first, first + count, 2):
        low, high = i % count, (i + 1) % count
        pairs += [(low, high), (high, low)]
    return lax.ppermute(value, axis, pairs)


def sent_whole(chunks, owners, capacity, width):
    count = len(chunks)
    stack = jnp.stack(chunks)
    rows = stack[:, :width].reshape(count, width // LANES, LANES, LANES)
    rows = rows.transpose(0, 2, 1, 3).reshape(owners, capacity, width)
    aims = stack[:, width:].transpose(0, 2, 1).reshape(owners, capacity, AIM_ROWS)
    rows, aims = (
        lax.all_to_all(part, ("lat", "lon"), split_axis=0, concat_axis=0, tiled=True)
        for part in (rows, aims)
    )
    rows = rows.reshape(count, LANES, width // LANES, LANES).transpose(0, 2, 1, 3)
    aims = aims.reshape(count, LANES, AIM_ROWS).transpose(0, 2, 1)
    stack = jnp.concatenate([rows.reshape(count, width, LANES), aims], axis=1)
    return [stack[i] for i in range(count)]


def per_device(
    grid_latent,
    grid_owner,
    grid_target,
    mesh_latent,
    edge_latent,
    mesh_sender,
    mesh_receiver,
    halo_rows,
    weights,
    biases,
    gains,
):
    rows_dev, width = grid_latent.shape
    nodes = mesh_latent.shape[0]
    edges = edge_latent.shape[0]
    lon_count = lax.axis_size("lon")
    owners = lax.axis_size("lat") * lon_count
    capacity = max(2, 2 * rows_dev // owners)
    exchange = capacity == LANES and owners <= 16

    other = swap(weights, "ch", 1)

    count = owners * capacity // LANES
    chunk_shape = ((width + AIM_ROWS, LANES), BF16)
    order = [2, 6, 1, 7, 3, 4, 5] if owners == 8 else list(range(1, count))
    lead, place, aims = call(
        functools.partial(place_kernel, owners, capacity, exchange, order[0]),
        [chunk_shape, ((1, rows_dev), jnp.int32), ((AIM_ROWS, rows_dev), BF16)],
        [
            pltpu.with_memory_space_constraint(value, pltpu.HBM)
            for value in (grid_owner.T, grid_target.T, grid_latent)
        ],
        [HBM] * 3,
        [
            pltpu.VMEM((1, rows_dev), jnp.int32),
            pltpu.VMEM((2, rows_dev), jnp.int32),
            pltpu.VMEM((rows_dev, width), BF16),
            pltpu.SemaphoreType.DMA((3,)),
        ],
        flops=10**9,
        moved=2 * 10**6,
    )
    others = [*order[1:], 0]
    chunks = {order[0]: lead}
    rest = call(
        functools.partial(dispatch_kernel, capacity, exchange, others),
        [chunk_shape] * len(others),
        (place, aims, grid_latent),
        [VMEM] * 3,
        flops=10**9,
        moved=2 * 10**6,
    )
    chunks.update(zip(others, rest))
    if exchange:
        arrived = {0: chunks[0]}
        for step in order:
            arrived[step] = moved(chunks[step], step)
        groups = [[0], order[:3], order[3:5], *[[step] for step in order[5:]]]
    else:
        arrived = dict(enumerate(sent_whole([chunks[i] for i in range(count)], owners, capacity, width)))
        groups = [[0], list(range(1, count))]

    total, part, ahead = call(
        first_kernel,
        [((nodes, width), F32), ((nodes, width), BF16), ((nodes, width), F32)],
        (weights, other, mesh_latent, arrived[0], biases),
        [VMEM] * 5,
        flops=5 * 10**8,
        moved=3 * 10**6,
    )
    for group in groups[1:-1]:
        (total,) = call(
            more_kernel,
            [((nodes, width), F32)],
            (total, part, weights, other, biases, *[arrived[i] for i in group]),
            [VMEM] * (5 + len(group)),
            flops=4 * 10**8 * len(group),
            moved=2 * 10**6,
        )
    mid, lent = call(
        node_kernel,
        [((nodes, width), BF16), ((halo_rows.shape[0], width), BF16)],
        (total, part, ahead, weights, other, biases, gains, mesh_latent)
        + (halo_rows.reshape(1, -1), *[arrived[i] for i in groups[-1]]),
        [VMEM] * (9 + len(groups[-1])),
        flops=10**9,
        moved=3 * 10**6,
    )
    halo = [paired(lent, "lat", 1), paired(lent, "lat", 0), shift(lent, "lon", 1)]
    if lon_count != 2:
        halo.append(shift(lent, "lon", -1))
    sender, receiver = mesh_sender.reshape(1, -1), mesh_receiver.reshape(1, -1)
    pieces, depth = len(halo), halo_rows.shape[0]
    pre, ahead, picks, spread = call(
        functools.partial(local_kernel, pieces, depth),
        [
            ((edges, width), F32),
            ((nodes, width), F32),
            ((edges, pieces * depth), BF16),
            ((nodes, edges), BF16),
        ],
        (mid, edge_latent, sender, receiver, biases, weights, other),
        [VMEM] * 7,
        flops=10**9,
        moved=3 * 10**6,
    )
    (out,) = call(
        process_kernel,
        [((nodes, width), BF16)],
        (pre, ahead, picks, spread, mid, gains, weights, other, *halo),
        [VMEM] * (8 + pieces),
        flops=10**9,
        moved=3 * 10**6,
    )
    return out


def solution(mesh):
    in_specs = (
        P(("member", "lat", "lon", "ch"), None),
        P(("member", "lat", "lon", "ch"), None),
        P(("member", "lat", "lon", "ch"), None),
        P(("member", "lat", "lon", "ch"), None),
        P(("member", "lat", "lon", "ch"), None),
        P(("member", "lat", "lon", "ch")),
        P(("member", "lat", "lon", "ch")),
        P(("member", "lat", "lon", "ch")),
        P(None, "ch", None),
        P(),
        P(),
    )
    out_specs = P(("member", "lat", "lon", "ch"), None)
    return jax.shard_map(
        per_device, mesh=mesh, in_specs=in_specs, out_specs=out_specs, check_vma=False
    )
```

```python
import functools

import jax
import jax.numpy as jnp
from jax import lax
from jax.experimental import pallas as pl
from jax.experimental.pallas import tpu as pltpu
from jax.sharding import PartitionSpec as P

EPSILON = 1e-05
LANES = 128
AIM_ROWS = 8
F32 = jnp.float32
BF16 = jnp.bfloat16
HBM = pl.BlockSpec(memory_space=pltpu.HBM)
VMEM = pl.BlockSpec(memory_space=pltpu.VMEM)
VMEM_LIMIT = 24 * 1024 * 1024


def mm(left, right):
    return jnp.dot(left, right, preferred_element_type=F32)


def mm_nt(left, right):
    return lax.dot_general(left, right, (((1,), (1,)), ((), ())), preferred_element_type=F32)


def silu(values):
    half = 0.5 * values
    return (half + half * jnp.tanh(half)).astype(BF16)


def normed(values):
    middle = jnp.mean(values, axis=-1, keepdims=True)
    centred = values - middle
    spread = jnp.mean(centred * centred, axis=-1, keepdims=True)
    return centred * lax.rsqrt(spread + EPSILON)


def as_bf16(mask):
    return jnp.where(mask, 1.0, 0.0).astype(BF16)


def down(row, count):
    return as_bf16(lax.broadcasted_iota(jnp.int32, (count, row.shape[1]), 0) == row)


def along(column, count):
    return as_bf16(lax.broadcasted_iota(jnp.int32, (column.shape[0], count), 1) == column)


def turned(row):
    wide = jnp.broadcast_to(row.astype(F32), (8, row.shape[1]))
    return jnp.transpose(wide)[:, :1].astype(jnp.int32)


def halves(rows):
    half = rows.shape[1] // 2
    low, high = rows[:, :half], rows[:, half:]
    first = lax.axis_index("ch") == 0
    return jnp.where(first, low, high), jnp.where(first, high, low)


def through(rows, maps, pick):
    here, there = halves(rows)
    return mm(here, maps[0][pick]) + mm(there, maps[1][pick])


def packed(place, aims, latent, base, out):
    rows, width = latent.shape
    pick = as_bf16(lax.broadcasted_iota(jnp.int32, (LANES, rows), 0) + base == place)
    data = mm(pick, latent).astype(BF16)
    for j in range(width // LANES):
        out[j * LANES : (j + 1) * LANES, :] = data[:, j * LANES : (j + 1) * LANES]
    out[width : width + AIM_ROWS, :] = mm_nt(aims, pick).astype(BF16)


def base_of(step, capacity, exchange):
    if not exchange:
        return step * LANES
    lats, lons = lax.axis_size("lat"), lax.axis_size("lon")
    lat, lon = lax.axis_index("lat"), lax.axis_index("lon")
    owner = lax.rem(lat + step // lons, lats) * lons + lax.rem(lon + step % lons, lons)
    return owner * capacity


def place_kernel(owners, capacity, exchange, step, owner_in, target_in, latent_in, *rest):
    out, place_out, aims_out, owner_ref, target_ref, latent_ref, sems = rest
    rows, width = latent_ref.shape
    pairs = ((owner_in, owner_ref), (target_in, target_ref), (latent_in, latent_ref))
    copies = [pltpu.make_async_copy(*pair, sems.at[i]) for i, pair in enumerate(pairs)]
    for copy in copies:
        copy.start()
    number = lax.broadcasted_iota(jnp.int32, (max(16, owners), rows), 0)
    before = as_bf16(
        lax.broadcasted_iota(jnp.int32, (rows, rows), 0)
        < lax.broadcasted_iota(jnp.int32, (rows, rows), 1)
    )
    copies[0].wait()
    named = number == owner_ref[...]
    rank = mm(as_bf16(named), before).astype(jnp.int32)
    place = jnp.sum(jnp.where(named, number * capacity + rank, 0), axis=0, keepdims=True)
    copies[1].wait()
    aims = jnp.concatenate(
        [
            (target_ref[...] + 1).astype(F32),
            jnp.zeros((AIM_ROWS - target_ref.shape[0], rows), F32),
        ],
        axis=0,
    ).astype(BF16)
    place_out[...] = place
    aims_out[...] = aims
    copies[2].wait()
    packed(place, aims, latent_ref[...], base_of(step, capacity, exchange), out)


def dispatch_kernel(capacity, exchange, steps, place_ref, aims_ref, latent_ref, *outs):
    place, aims, latent = place_ref[...], aims_ref[...], latent_ref[...]
    for step, out in zip(steps, outs):
        packed(place, aims, latent, base_of(step, capacity, exchange), out)


def encode(chunks, maps, mesh_part, bias):
    nodes, width = mesh_part.shape
    rows = jnp.concatenate(
        [
            jnp.concatenate(
                [chunk[j * LANES : (j + 1) * LANES, :] for j in range(width // LANES)], axis=1
            )
            for chunk in chunks
        ],
        axis=0,
    )
    lines = [chunk[width : width + AIM_ROWS, :].astype(F32) for chunk in chunks]
    columns = [jnp.transpose(line).astype(jnp.int32) - 1 for line in lines]
    lines = [line.astype(jnp.int32) - 1 for line in lines]
    part = through(rows, maps, 0) + bias
    picks = jnp.concatenate(
        [along(column[:, k : k + 1], nodes) for k in range(2) for column in columns], axis=0
    )
    spread = jnp.concatenate(
        [down(line[k : k + 1, :], nodes) for k in range(2) for line in lines], axis=1
    )
    hidden = silu(jnp.concatenate([part, part], axis=0) + mm(picks, mesh_part))
    return mm(spread, normed(through(hidden, maps, 2)).astype(BF16))


def first_kernel(mine, other, mesh, lend, biases, *rest):
    *chunks, sum_out, part_out, ahead_out, lent_ahead_out, lent_latent_out = rest
    maps = (mine, other)
    latent = mesh[...]
    part = through(latent, maps, 1).astype(BF16)
    part_out[...] = part
    ahead_out[...] = through(latent, maps, 3) + biases[1:2, :]
    lent = mm(along(turned(lend[...]), latent.shape[0]), latent).astype(BF16)
    lent_latent_out[...] = lent
    lent_ahead_out[...] = through(lent, maps, 3) + biases[1:2, :]
    sum_out[...] = encode(chunks, maps, part, biases[0:1, :])


def more_kernel(total, part, mine, other, biases, *rest):
    *chunks, out = rest
    out[...] = total[...] + encode(chunks, (mine, other), part[...], biases[0:1, :])


def node_kernel(total, part, ahead, mine, other, biases, gains, mesh, lend, *rest):
    *chunks, sums_out, lent_out = rest
    maps = (mine, other)
    sums = total[...] + encode(chunks, maps, part[...], biases[0:1, :])
    sums = (sums * gains[0:1, :]).astype(BF16)
    sums_out[...] = sums
    picks = along(turned(lend[...]), sums.shape[0])
    lent = mm(picks, sums).astype(BF16)
    lent_out[...] = updated(ahead[...], lent, mesh[...], maps, gains)


def updated(ahead, sums, latent, maps, gains):
    hidden = silu(ahead + through(sums, maps, 4))
    change = normed(through(hidden, maps, 5)) * gains[1:2, :]
    return (latent.astype(F32) + change).astype(BF16)


def local_kernel(pieces, depth, sums, node_ahead, mesh, edges, sender, receiver, *rest):
    biases, gains, mine, other, mid_out, pre_out, ahead_out, picks_out, spread_out = rest
    maps = (mine, other)
    mid = updated(node_ahead[...], sums[...], mesh[...], maps, gains)
    mid_out[...] = mid
    nodes = mid.shape[0]
    number = sender[...]
    entry = number - nodes
    if pieces == 3:
        entry = jnp.where(entry >= 3 * depth, entry - depth, entry)
    odd = lax.rem(lax.axis_index("lat"), 2) == 1
    crossed = jnp.where(entry < depth, entry + depth, jnp.where(entry < 2 * depth, entry - depth, entry))
    entry = jnp.where(odd & (entry >= 0), crossed, entry)
    picks_out[...] = along(turned(entry), pieces * depth)
    spread_out[...] = down(receiver[...], nodes)
    at_sender = along(turned(number), nodes)
    at_receiver = along(turned(receiver[...]), nodes)
    ahead_out[...] = through(mid, maps, 10) + biases[3:4, :]
    pre = through(edges[...], maps, 6) + biases[2:3, :]
    pre = pre + mm(at_sender, through(mid, maps, 7).astype(BF16))
    pre_out[...] = pre + mm(at_receiver, through(mid, maps, 8).astype(BF16))


def process_kernel(pre, ahead, picks, spread, mid, gains, mine, other, *rest):
    *lent, out = rest
    lent = [lent[1], lent[0], *lent[2:]]
    maps = (mine, other)
    table = jnp.concatenate([ref[...] for ref in lent], axis=0)
    hidden = silu(pre[...] + mm(picks[...], through(table, maps, 7).astype(BF16)))
    notes = normed(through(hidden, maps, 9)).astype(BF16)
    processed = (mm(spread[...], notes) * gains[2:3, :]).astype(BF16)
    hidden = silu(ahead[...] + through(processed, maps, 11))
    out[...] = (
        mid[...].astype(F32) + normed(through(hidden, maps, 12)) * gains[3:4, :]
    ).astype(BF16)


def call(kernel, outs, ins, specs, scratch=(), flops=0, moved=0):
    return pl.pallas_call(
        kernel,
        out_shape=[jax.ShapeDtypeStruct(shape, kind) for shape, kind in outs],
        in_specs=specs,
        out_specs=[VMEM] * len(outs),
        scratch_shapes=list(scratch),
        compiler_params=pltpu.CompilerParams(vmem_limit_bytes=VMEM_LIMIT),
        cost_estimate=pl.CostEstimate(flops=flops, bytes_accessed=moved, transcendentals=0),
    )(*ins)


def swap(value, axes, step):
    count = lax.axis_size(axes)
    return lax.ppermute(value, axes, [(i, i ^ step) for i in range(count)])


def moved(value, step):
    lats, lons = lax.axis_size("lat"), lax.axis_size("lon")
    pairs = []
    for i in range(lats * lons):
        lat, lon = (i // lons + step // lons) % lats, (i % lons + step % lons) % lons
        pairs.append((i, lat * lons + lon))
    return lax.ppermute(value, ("lat", "lon"), pairs)


def shift(value, axis, step):
    count = lax.axis_size(axis)
    return lax.ppermute(value, axis, [(i, (i + step) % count) for i in range(count)])


def paired(value, axis, first):
    count = lax.axis_size(axis)
    pairs = []
    for i in range(first, first + count, 2):
        low, high = i % count, (i + 1) % count
        pairs += [(low, high), (high, low)]
    return lax.ppermute(value, axis, pairs)


def sent_whole(chunks, owners, capacity, width):
    count = len(chunks)
    stack = jnp.stack(chunks)
    rows = stack[:, :width].reshape(count, width // LANES, LANES, LANES)
    rows = rows.transpose(0, 2, 1, 3).reshape(owners, capacity, width)
    aims = stack[:, width:].transpose(0, 2, 1).reshape(owners, capacity, AIM_ROWS)
    rows, aims = (
        lax.all_to_all(part, ("lat", "lon"), split_axis=0, concat_axis=0, tiled=True)
        for part in (rows, aims)
    )
    rows = rows.reshape(count, LANES, width // LANES, LANES).transpose(0, 2, 1, 3)
    aims = aims.reshape(count, LANES, AIM_ROWS).transpose(0, 2, 1)
    stack = jnp.concatenate([rows.reshape(count, width, LANES), aims], axis=1)
    return [stack[i] for i in range(count)]


def per_device(
    grid_latent,
    grid_owner,
    grid_target,
    mesh_latent,
    edge_latent,
    mesh_sender,
    mesh_receiver,
    halo_rows,
    weights,
    biases,
    gains,
):
    rows_dev, width = grid_latent.shape
    nodes = mesh_latent.shape[0]
    edges = edge_latent.shape[0]
    lon_count = lax.axis_size("lon")
    owners = lax.axis_size("lat") * lon_count
    capacity = max(2, 2 * rows_dev // owners)
    exchange = capacity == LANES and owners <= 16

    other = swap(weights, "ch", 1)

    count = owners * capacity // LANES
    chunk_shape = ((width + AIM_ROWS, LANES), BF16)
    order = [4, 2, 6, 1, 7, 3, 5] if owners == 8 else list(range(1, count))
    lead, place, aims = call(
        functools.partial(place_kernel, owners, capacity, exchange, order[0]),
        [chunk_shape, ((1, rows_dev), jnp.int32), ((AIM_ROWS, rows_dev), BF16)],
        [
            pltpu.with_memory_space_constraint(value, pltpu.HBM)
            for value in (grid_owner.T, grid_target.T, grid_latent)
        ],
        [HBM] * 3,
        [
            pltpu.VMEM((1, rows_dev), jnp.int32),
            pltpu.VMEM((2, rows_dev), jnp.int32),
            pltpu.VMEM((rows_dev, width), BF16),
            pltpu.SemaphoreType.DMA((3,)),
        ],
        flops=10**9,
        moved=2 * 10**6,
    )
    others = [*order[1:], 0]
    chunks = {order[0]: lead}
    rest = call(
        functools.partial(dispatch_kernel, capacity, exchange, others),
        [chunk_shape] * len(others),
        (place, aims, grid_latent),
        [VMEM] * 3,
        flops=10**9,
        moved=2 * 10**6,
    )
    chunks.update(zip(others, rest))
    if exchange:
        arrived = {0: chunks[0]}
        for step in order:
            arrived[step] = moved(chunks[step], step)
        groups = [[0, order[0]], order[1:3], order[3:5], *[[step] for step in order[5:]]]
    else:
        arrived = dict(enumerate(sent_whole([chunks[i] for i in range(count)], owners, capacity, width)))
        groups = [[0], list(range(1, count))]

    depth = halo_rows.shape[0]
    lend = halo_rows.reshape(1, -1)
    total, part, node_ahead, lent_ahead, lent_latent = call(
        first_kernel,
        [((nodes, width), F32), ((nodes, width), BF16), ((nodes, width), F32)]
        + [((depth, width), F32), ((depth, width), BF16)],
        (weights, other, mesh_latent, lend, biases, *[arrived[i] for i in groups[0]]),
        [VMEM] * (5 + len(groups[0])),
        flops=5 * 10**8,
        moved=3 * 10**6,
    )
    for group in groups[1:-1]:
        (total,) = call(
            more_kernel,
            [((nodes, width), F32)],
            (total, part, weights, other, biases, *[arrived[i] for i in group]),
            [VMEM] * (5 + len(group)),
            flops=4 * 10**8 * len(group),
            moved=2 * 10**6,
        )
    sums, lent = call(
        node_kernel,
        [((nodes, width), BF16), ((depth, width), BF16)],
        (total, part, lent_ahead, weights, other, biases, gains, lent_latent)
        + (lend, *[arrived[i] for i in groups[-1]]),
        [VMEM] * (9 + len(groups[-1])),
        flops=10**9,
        moved=3 * 10**6,
    )
    halo = [paired(lent, "lat", 1), paired(lent, "lat", 0), shift(lent, "lon", 1)]
    if lon_count != 2:
        halo.append(shift(lent, "lon", -1))
    sender, receiver = mesh_sender.reshape(1, -1), mesh_receiver.reshape(1, -1)
    pieces = len(halo)
    mid, pre, ahead, picks, spread = call(
        functools.partial(local_kernel, pieces, depth),
        [
            ((nodes, width), BF16),
            ((edges, width), F32),
            ((nodes, width), F32),
            ((edges, pieces * depth), BF16),
            ((nodes, edges), BF16),
        ],
        (sums, node_ahead, mesh_latent, edge_latent, sender, receiver)
        + (biases, gains, weights, other),
        [VMEM] * 10,
        flops=10**9,
        moved=3 * 10**6,
    )
    (out,) = call(
        process_kernel,
        [((nodes, width), BF16)],
        (pre, ahead, picks, spread, mid, gains, weights, other, halo[1], halo[0], *halo[2:]),
        [VMEM] * (8 + pieces),
        flops=10**9,
        moved=3 * 10**6,
    )
    return out


def solution(mesh):
    in_specs = (
        P(("member", "lat", "lon", "ch"), None),
        P(("member", "lat", "lon", "ch"), None),
        P(("member", "lat", "lon", "ch"), None),
        P(("member", "lat", "lon", "ch"), None),
        P(("member", "lat", "lon", "ch"), None),
        P(("member", "lat", "lon", "ch")),
        P(("member", "lat", "lon", "ch")),
        P(("member", "lat", "lon", "ch")),
        P(None, "ch", None),
        P(),
        P(),
    )
    out_specs = P(("member", "lat", "lon", "ch"), None)
    return jax.shard_map(
        per_device, mesh=mesh, in_specs=in_specs, out_specs=out_specs, check_vma=False
    )
```

```python
import functools

import jax
import jax.numpy as jnp
from jax import lax
from jax.experimental import pallas as pl
from jax.experimental.pallas import tpu as pltpu
from jax.sharding import PartitionSpec as P

EPSILON = 1e-05
LANES = 128
AIM_ROWS = 8
F32 = jnp.float32
BF16 = jnp.bfloat16
HBM = pl.BlockSpec(memory_space=pltpu.HBM)
ANY = pl.BlockSpec(memory_space=pl.ANY)
VMEM = pl.BlockSpec(memory_space=pltpu.VMEM)
VMEM_LIMIT = 24 * 1024 * 1024


def mm(left, right):
    return jnp.dot(left, right, preferred_element_type=F32)


def mm_nt(left, right):
    return lax.dot_general(left, right, (((1,), (1,)), ((), ())), preferred_element_type=F32)


def silu(values):
    half = 0.5 * values
    return (half + half * jnp.tanh(half)).astype(BF16)


def normed(values):
    middle = jnp.mean(values, axis=-1, keepdims=True)
    centred = values - middle
    spread = jnp.mean(centred * centred, axis=-1, keepdims=True)
    return centred * lax.rsqrt(spread + EPSILON)


def as_bf16(mask):
    return jnp.where(mask, 1.0, 0.0).astype(BF16)


def down(row, count):
    return as_bf16(lax.broadcasted_iota(jnp.int32, (count, row.shape[1]), 0) == row)


def along(column, count):
    return as_bf16(lax.broadcasted_iota(jnp.int32, (column.shape[0], count), 1) == column)


def turned(row):
    wide = jnp.broadcast_to(row.astype(F32), (8, row.shape[1]))
    return jnp.transpose(wide)[:, :1].astype(jnp.int32)


def halves(rows):
    half = rows.shape[1] // 2
    low, high = rows[:, :half], rows[:, half:]
    first = lax.axis_index("ch") == 0
    return jnp.where(first, low, high), jnp.where(first, high, low)


def through(rows, maps, pick):
    here, there = halves(rows)
    return mm(here, maps[0][pick]) + mm(there, maps[1][pick])


def packed(place, aims, latent, base, out):
    rows, width = latent.shape
    pick = as_bf16(lax.broadcasted_iota(jnp.int32, (LANES, rows), 0) + base == place)
    data = mm(pick, latent).astype(BF16)
    for j in range(width // LANES):
        out[j * LANES : (j + 1) * LANES, :] = data[:, j * LANES : (j + 1) * LANES]
    out[width : width + AIM_ROWS, :] = mm_nt(aims, pick).astype(BF16)


def base_of(step, capacity, exchange):
    if not exchange:
        return step * LANES
    lats, lons = lax.axis_size("lat"), lax.axis_size("lon")
    lat, lon = lax.axis_index("lat"), lax.axis_index("lon")
    owner = lax.rem(lat + step // lons, lats) * lons + lax.rem(lon + step % lons, lons)
    return owner * capacity


def place_kernel(owners, capacity, exchange, step, owner_in, target_in, latent_in, *rest):
    out, place_out, aims_out, owner_ref, target_ref, latent_ref, sems = rest
    rows, width = latent_ref.shape
    pairs = ((owner_in, owner_ref), (target_in, target_ref), (latent_in, latent_ref))
    copies = [pltpu.make_async_copy(*pair, sems.at[i]) for i, pair in enumerate(pairs)]
    for copy in copies:
        copy.start()
    number = lax.broadcasted_iota(jnp.int32, (max(16, owners), rows), 0)
    before = as_bf16(
        lax.broadcasted_iota(jnp.int32, (rows, rows), 0)
        < lax.broadcasted_iota(jnp.int32, (rows, rows), 1)
    )
    copies[0].wait()
    named = number == owner_ref[...]
    rank = mm(as_bf16(named), before).astype(jnp.int32)
    place = jnp.sum(jnp.where(named, number * capacity + rank, 0), axis=0, keepdims=True)
    copies[1].wait()
    aims = jnp.concatenate(
        [
            (target_ref[...] + 1).astype(F32),
            jnp.zeros((AIM_ROWS - target_ref.shape[0], rows), F32),
        ],
        axis=0,
    ).astype(BF16)
    place_out[...] = place
    aims_out[...] = aims
    copies[2].wait()
    packed(place, aims, latent_ref[...], base_of(step, capacity, exchange), out)


def dispatch_kernel(capacity, exchange, steps, place_ref, aims_ref, latent_ref, after, *outs):
    del after
    place, aims, latent = place_ref[...], aims_ref[...], latent_ref[...]
    for step, out in zip(steps, outs):
        packed(place, aims, latent, base_of(step, capacity, exchange), out)


def messages(chunks, maps, mesh_part, bias):
    nodes, width = mesh_part.shape
    rows = jnp.concatenate(
        [
            jnp.concatenate(
                [chunk[j * LANES : (j + 1) * LANES, :] for j in range(width // LANES)], axis=1
            )
            for chunk in chunks
        ],
        axis=0,
    )
    lines = [chunk[width : width + AIM_ROWS, :].astype(F32) for chunk in chunks]
    columns = [jnp.transpose(line).astype(jnp.int32) - 1 for line in lines]
    lines = [line.astype(jnp.int32) - 1 for line in lines]
    part = through(rows, maps, 0) + bias
    picks = jnp.concatenate(
        [along(column[:, k : k + 1], nodes) for k in range(2) for column in columns], axis=0
    )
    spread = jnp.concatenate(
        [down(line[k : k + 1, :], nodes) for k in range(2) for line in lines], axis=1
    )
    hidden = silu(jnp.concatenate([part, part], axis=0) + mm(picks, mesh_part))
    return spread, normed(through(hidden, maps, 2)).astype(BF16)


def encode(chunks, maps, mesh_part, bias):
    return mm(*messages(chunks, maps, mesh_part, bias))


def rows_of(picks, values):
    parts = []
    for _ in range(3):
        parts.append(values.astype(BF16))
        values = values - parts[-1].astype(F32)
    return sum(mm(picks, part) for part in parts)


def first_kernel(mine, other, mesh, lend, biases, *rest):
    *chunks, sum_out, part_out, ahead_out, lent_ahead_out, lent_latent_out = rest
    maps = (mine, other)
    latent = mesh[...]
    part = through(latent, maps, 1).astype(BF16)
    part_out[...] = part
    ahead_out[...] = through(latent, maps, 3) + biases[1:2, :]
    lent = mm(along(turned(lend[...]), latent.shape[0]), latent).astype(BF16)
    lent_latent_out[...] = lent
    lent_ahead_out[...] = through(lent, maps, 3) + biases[1:2, :]
    sum_out[...] = encode(chunks, maps, part, biases[0:1, :])


def more_kernel(total, part, mine, other, biases, *rest):
    *chunks, out = rest
    out[...] = total[...] + encode(chunks, (mine, other), part[...], biases[0:1, :])


def last_kernel(total, part, mine, other, biases, lend, *rest):
    *chunks, out, lent_out = rest
    sums = total[...] + encode(chunks, (mine, other), part[...], biases[0:1, :])
    out[...] = sums
    lent_out[...] = rows_of(along(turned(lend[...]), sums.shape[0]), sums)


def node_kernel(lent_total, part, ahead, mine, other, biases, gains, latent, lend, *rest):
    *chunks, spread_out, notes_out, lent_out = rest
    maps = (mine, other)
    spread, notes = messages(chunks, maps, part[...], biases[0:1, :])
    spread_out[...] = spread
    notes_out[...] = notes
    lent_spread = mm(along(turned(lend[...]), spread.shape[0]), spread).astype(BF16)
    sums = ((lent_total[...] + mm(lent_spread, notes)) * gains[0:1, :]).astype(BF16)
    mid = updated(ahead[...], sums, latent[...], maps, gains)
    lent_out[...] = through(mid, maps, 7).astype(BF16)


def updated(ahead, sums, latent, maps, gains):
    hidden = silu(ahead + through(sums, maps, 4))
    change = normed(through(hidden, maps, 5)) * gains[1:2, :]
    return (latent.astype(F32) + change).astype(BF16)


def local_kernel(pieces, depth, total, spread, notes, node_ahead, mesh, edges, sender, receiver, *rest):
    biases, gains, mine, other, mid_out, pre_out, ahead_out, picks_out, spread_out = rest
    maps = (mine, other)
    sums = ((total[...] + mm(spread[...], notes[...])) * gains[0:1, :]).astype(BF16)
    mid = updated(node_ahead[...], sums, mesh[...], maps, gains)
    mid_out[...] = mid
    nodes = mid.shape[0]
    number = sender[...]
    entry = number - nodes
    if pieces == 3:
        entry = jnp.where(entry >= 3 * depth, entry - depth, entry)
    odd = lax.rem(lax.axis_index("lat"), 2) == 1
    crossed = jnp.where(entry < depth, entry + depth, jnp.where(entry < 2 * depth, entry - depth, entry))
    entry = jnp.where(odd & (entry >= 0), crossed, entry)
    picks_out[...] = along(turned(entry), pieces * depth)
    spread_out[...] = down(receiver[...], nodes)
    at_sender = along(turned(number), nodes)
    at_receiver = along(turned(receiver[...]), nodes)
    ahead_out[...] = through(mid, maps, 10) + biases[3:4, :]
    pre = through(edges[...], maps, 6) + biases[2:3, :]
    pre = pre + mm(at_sender, through(mid, maps, 7).astype(BF16))
    pre_out[...] = pre + mm(at_receiver, through(mid, maps, 8).astype(BF16))


def process_kernel(pre, ahead, picks, spread, mid, gains, mine, other, *rest):
    *lent, out = rest
    lent = [lent[1], lent[0], *lent[2:]]
    maps = (mine, other)
    table = jnp.concatenate([ref[...] for ref in lent], axis=0)
    hidden = silu(pre[...] + mm(picks[...], table))
    notes = normed(through(hidden, maps, 9)).astype(BF16)
    processed = (mm(spread[...], notes) * gains[2:3, :]).astype(BF16)
    hidden = silu(ahead[...] + through(processed, maps, 11))
    out[...] = (
        mid[...].astype(F32) + normed(through(hidden, maps, 12)) * gains[3:4, :]
    ).astype(BF16)


def call(kernel, outs, ins, specs, scratch=(), flops=0, moved=0):
    return pl.pallas_call(
        kernel,
        out_shape=[jax.ShapeDtypeStruct(shape, kind) for shape, kind in outs],
        in_specs=specs,
        out_specs=[VMEM] * len(outs),
        scratch_shapes=list(scratch),
        compiler_params=pltpu.CompilerParams(vmem_limit_bytes=VMEM_LIMIT),
        cost_estimate=pl.CostEstimate(flops=flops, bytes_accessed=moved, transcendentals=0),
    )(*ins)


def swap(value, axes, step):
    count = lax.axis_size(axes)
    return lax.ppermute(value, axes, [(i, i ^ step) for i in range(count)])


def moved(value, step):
    lats, lons = lax.axis_size("lat"), lax.axis_size("lon")
    pairs = []
    for i in range(lats * lons):
        lat, lon = (i // lons + step // lons) % lats, (i % lons + step % lons) % lons
        pairs.append((i, lat * lons + lon))
    return lax.ppermute(value, ("lat", "lon"), pairs)


def shift(value, axis, step):
    count = lax.axis_size(axis)
    return lax.ppermute(value, axis, [(i, (i + step) % count) for i in range(count)])


def paired(value, axis, first):
    count = lax.axis_size(axis)
    pairs = []
    for i in range(first, first + count, 2):
        low, high = i % count, (i + 1) % count
        pairs += [(low, high), (high, low)]
    return lax.ppermute(value, axis, pairs)


def sent_whole(chunks, owners, capacity, width):
    count = len(chunks)
    stack = jnp.stack(chunks)
    rows = stack[:, :width].reshape(count, width // LANES, LANES, LANES)
    rows = rows.transpose(0, 2, 1, 3).reshape(owners, capacity, width)
    aims = stack[:, width:].transpose(0, 2, 1).reshape(owners, capacity, AIM_ROWS)
    rows, aims = (
        lax.all_to_all(part, ("lat", "lon"), split_axis=0, concat_axis=0, tiled=True)
        for part in (rows, aims)
    )
    rows = rows.reshape(count, LANES, width // LANES, LANES).transpose(0, 2, 1, 3)
    aims = aims.reshape(count, LANES, AIM_ROWS).transpose(0, 2, 1)
    stack = jnp.concatenate([rows.reshape(count, width, LANES), aims], axis=1)
    return [stack[i] for i in range(count)]


def per_device(
    grid_latent,
    grid_owner,
    grid_target,
    mesh_latent,
    edge_latent,
    mesh_sender,
    mesh_receiver,
    halo_rows,
    weights,
    biases,
    gains,
):
    rows_dev, width = grid_latent.shape
    nodes = mesh_latent.shape[0]
    edges = edge_latent.shape[0]
    lon_count = lax.axis_size("lon")
    owners = lax.axis_size("lat") * lon_count
    capacity = max(2, 2 * rows_dev // owners)
    exchange = capacity == LANES and owners <= 16

    other = swap(weights, "ch", 1)

    count = owners * capacity // LANES
    chunk_shape = ((width + AIM_ROWS, LANES), BF16)
    order = [4, 2, 6, 1, 7, 3, 5] if owners == 8 else list(range(1, count))
    lead, place, aims = call(
        functools.partial(place_kernel, owners, capacity, exchange, order[0]),
        [chunk_shape, ((1, rows_dev), jnp.int32), ((AIM_ROWS, rows_dev), BF16)],
        [
            pltpu.with_memory_space_constraint(value, pltpu.HBM)
            for value in (grid_owner.T, grid_target.T, grid_latent)
        ],
        [HBM] * 3,
        [
            pltpu.VMEM((1, rows_dev), jnp.int32),
            pltpu.VMEM((2, rows_dev), jnp.int32),
            pltpu.VMEM((rows_dev, width), BF16),
            pltpu.SemaphoreType.DMA((3,)),
        ],
        flops=10**9,
        moved=2 * 10**6,
    )
    chunks = {order[0]: lead}
    early, late = order[1:4], [*order[4:], 0]
    for steps, after in ((early, aims), (late, other)):
        made = call(
            functools.partial(dispatch_kernel, capacity, exchange, steps),
            [chunk_shape] * len(steps),
            (place, aims, grid_latent, after),
            [VMEM] * 3 + [ANY],
            flops=10**9,
            moved=2 * 10**6,
        )
        chunks.update(zip(steps, made))
    if exchange:
        arrived = {0: chunks[0]}
        for step in order:
            arrived[step] = moved(chunks[step], step)
        groups = [[0, 4], [2, 6], [1, 7], [3], [5]]
    else:
        arrived = dict(enumerate(sent_whole([chunks[i] for i in range(count)], owners, capacity, width)))
        groups = [[0], [1], list(range(2, count))]

    depth = halo_rows.shape[0]
    lend = halo_rows.reshape(1, -1)
    total, part, node_ahead, lent_ahead, lent_latent = call(
        first_kernel,
        [((nodes, width), F32), ((nodes, width), BF16), ((nodes, width), F32)]
        + [((depth, width), F32), ((depth, width), BF16)],
        (weights, other, mesh_latent, lend, biases, *[arrived[i] for i in groups[0]]),
        [VMEM] * (5 + len(groups[0])),
        flops=5 * 10**8,
        moved=3 * 10**6,
    )
    for group in groups[1:-2]:
        (total,) = call(
            more_kernel,
            [((nodes, width), F32)],
            (total, part, weights, other, biases, *[arrived[i] for i in group]),
            [VMEM] * (5 + len(group)),
            flops=4 * 10**8 * len(group),
            moved=2 * 10**6,
        )
    total, lent_total = call(
        last_kernel,
        [((nodes, width), F32), ((depth, width), F32)],
        (total, part, weights, other, biases, lend, *[arrived[i] for i in groups[-2]]),
        [VMEM] * (6 + len(groups[-2])),
        flops=10**9,
        moved=2 * 10**6,
    )
    last_edges = 2 * LANES * len(groups[-1])
    spread, notes, lent = call(
        node_kernel,
        [((nodes, last_edges), BF16), ((last_edges, width), BF16), ((depth, width), BF16)],
        (lent_total, part, lent_ahead, weights, other, biases, gains, lent_latent)
        + (lend, *[arrived[i] for i in groups[-1]]),
        [VMEM] * (9 + len(groups[-1])),
        flops=10**9,
        moved=3 * 10**6,
    )
    halo = [paired(lent, "lat", 1), paired(lent, "lat", 0), shift(lent, "lon", 1)]
    if lon_count != 2:
        halo.append(shift(lent, "lon", -1))
    sender, receiver = mesh_sender.reshape(1, -1), mesh_receiver.reshape(1, -1)
    pieces = len(halo)
    mid, pre, ahead, picks, spread = call(
        functools.partial(local_kernel, pieces, depth),
        [
            ((nodes, width), BF16),
            ((edges, width), F32),
            ((nodes, width), F32),
            ((edges, pieces * depth), BF16),
            ((nodes, edges), BF16),
        ],
        (total, spread, notes, node_ahead, mesh_latent, edge_latent, sender, receiver)
        + (biases, gains, weights, other),
        [VMEM] * 12,
        flops=10**9,
        moved=3 * 10**6,
    )
    (out,) = call(
        process_kernel,
        [((nodes, width), BF16)],
        (pre, ahead, picks, spread, mid, gains, weights, other, halo[1], halo[0], *halo[2:]),
        [VMEM] * (8 + pieces),
        flops=10**9,
        moved=3 * 10**6,
    )
    return out


def solution(mesh):
    in_specs = (
        P(("member", "lat", "lon", "ch"), None),
        P(("member", "lat", "lon", "ch"), None),
        P(("member", "lat", "lon", "ch"), None),
        P(("member", "lat", "lon", "ch"), None),
        P(("member", "lat", "lon", "ch"), None),
        P(("member", "lat", "lon", "ch")),
        P(("member", "lat", "lon", "ch")),
        P(("member", "lat", "lon", "ch")),
        P(None, "ch", None),
        P(),
        P(),
    )
    out_specs = P(("member", "lat", "lon", "ch"), None)
    return jax.shard_map(
        per_device, mesh=mesh, in_specs=in_specs, out_specs=out_specs, check_vma=False
    )
```

```python
import functools

import jax
import jax.numpy as jnp
from jax import lax
from jax.experimental import pallas as pl
from jax.experimental.pallas import tpu as pltpu
from jax.sharding import PartitionSpec as P

EPSILON = 1e-05
LANES = 128
AIM_ROWS = 16
F32 = jnp.float32
BF16 = jnp.bfloat16
HBM = pl.BlockSpec(memory_space=pltpu.HBM)
ANY = pl.BlockSpec(memory_space=pl.ANY)
VMEM = pl.BlockSpec(memory_space=pltpu.VMEM)
VMEM_LIMIT = 24 * 1024 * 1024


def mm(left, right):
    return jnp.dot(left, right, preferred_element_type=F32)


def mm_nt(left, right):
    return lax.dot_general(left, right, (((1,), (1,)), ((), ())), preferred_element_type=F32)


def silu(values):
    half = 0.5 * values
    return (half + half * jnp.tanh(half)).astype(BF16)


def normed(values):
    middle = jnp.mean(values, axis=-1, keepdims=True)
    centred = values - middle
    spread = jnp.mean(centred * centred, axis=-1, keepdims=True)
    return centred * lax.rsqrt(spread + EPSILON)


def as_bf16(mask):
    return jnp.where(mask, 1.0, 0.0).astype(BF16)


def down(row, count):
    return as_bf16(lax.broadcasted_iota(jnp.int32, (count, row.shape[1]), 0) == row)


def along(column, count):
    return as_bf16(lax.broadcasted_iota(jnp.int32, (column.shape[0], count), 1) == column)


def turned(row):
    wide = jnp.broadcast_to(row.astype(F32), (8, row.shape[1]))
    return jnp.transpose(wide)[:, :1].astype(jnp.int32)


def halves(rows):
    half = rows.shape[1] // 2
    low, high = rows[:, :half], rows[:, half:]
    first = lax.axis_index("ch") == 0
    return jnp.where(first, low, high), jnp.where(first, high, low)


def through(rows, maps, pick):
    here, there = halves(rows)
    return mm(here, maps[0][pick]) + mm(there, maps[1][pick])


def packed(place, aims, latent, base, out):
    rows, width = latent.shape
    pick = as_bf16(lax.broadcasted_iota(jnp.int32, (LANES, rows), 0) + base == place)
    data = mm(pick, latent).astype(BF16)
    for j in range(width // LANES):
        out[j * LANES : (j + 1) * LANES, :] = data[:, j * LANES : (j + 1) * LANES]
    out[width : width + AIM_ROWS, :] = mm_nt(aims, pick).astype(BF16)


def base_of(step, capacity, exchange):
    if not exchange:
        return step * LANES
    lats, lons = lax.axis_size("lat"), lax.axis_size("lon")
    lat, lon = lax.axis_index("lat"), lax.axis_index("lon")
    owner = lax.rem(lat + step // lons, lats) * lons + lax.rem(lon + step % lons, lons)
    return owner * capacity


def place_kernel(owners, capacity, exchange, step, owner_in, target_in, latent_in, *rest):
    out, place_out, aims_out, owner_ref, target_ref, latent_ref, sems = rest
    rows, width = latent_ref.shape
    pairs = ((owner_in, owner_ref), (target_in, target_ref), (latent_in, latent_ref))
    copies = [pltpu.make_async_copy(*pair, sems.at[i]) for i, pair in enumerate(pairs)]
    for copy in copies:
        copy.start()
    number = lax.broadcasted_iota(jnp.int32, (max(16, owners), rows), 0)
    before = as_bf16(
        lax.broadcasted_iota(jnp.int32, (rows, rows), 0)
        < lax.broadcasted_iota(jnp.int32, (rows, rows), 1)
    )
    copies[0].wait()
    named = number == owner_ref[...]
    rank = mm(as_bf16(named), before).astype(jnp.int32)
    place = jnp.sum(jnp.where(named, number * capacity + rank, 0), axis=0, keepdims=True)
    copies[1].wait()
    aims = jnp.concatenate(
        [
            (target_ref[...] + 1).astype(F32),
            jnp.zeros((AIM_ROWS - target_ref.shape[0], rows), F32),
        ],
        axis=0,
    ).astype(BF16)
    place_out[...] = place
    aims_out[...] = aims
    copies[2].wait()
    packed(place, aims, latent_ref[...], base_of(step, capacity, exchange), out)


def dispatch_kernel(capacity, exchange, steps, place_ref, aims_ref, latent_ref, after, *outs):
    del after
    place, aims, latent = place_ref[...], aims_ref[...], latent_ref[...]
    for step, out in zip(steps, outs):
        packed(place, aims, latent, base_of(step, capacity, exchange), out)


def messages(chunks, maps, mesh_part, bias):
    nodes, width = mesh_part.shape
    rows = jnp.concatenate(
        [
            jnp.concatenate(
                [chunk[j * LANES : (j + 1) * LANES, :] for j in range(width // LANES)], axis=1
            )
            for chunk in chunks
        ],
        axis=0,
    )
    lines = [chunk[width : width + AIM_ROWS, :].astype(F32) for chunk in chunks]
    columns = [jnp.transpose(line).astype(jnp.int32) - 1 for line in lines]
    lines = [line.astype(jnp.int32) - 1 for line in lines]
    part = through(rows, maps, 0) + bias
    picks = jnp.concatenate(
        [along(column[:, k : k + 1], nodes) for k in range(2) for column in columns], axis=0
    )
    spread = jnp.concatenate(
        [down(line[k : k + 1, :], nodes) for k in range(2) for line in lines], axis=1
    )
    hidden = silu(jnp.concatenate([part, part], axis=0) + mm(picks, mesh_part))
    return spread, normed(through(hidden, maps, 2)).astype(BF16)


def encode(chunks, maps, mesh_part, bias):
    return mm(*messages(chunks, maps, mesh_part, bias))


def rows_of(picks, values):
    parts = []
    for _ in range(3):
        parts.append(values.astype(BF16))
        values = values - parts[-1].astype(F32)
    return sum(mm(picks, part) for part in parts)


def edge_ends(pieces, depth, nodes, sender, receiver):
    entry = sender - nodes
    if pieces == 3:
        entry = jnp.where(entry >= 3 * depth, entry - depth, entry)
    odd = lax.rem(lax.axis_index("lat"), 2) == 1
    crossed = jnp.where(entry < 2 * depth, entry - depth, entry)
    crossed = jnp.where(entry < depth, entry + depth, crossed)
    entry = jnp.where(odd & (entry >= 0), crossed, entry)
    return (
        along(turned(entry), pieces * depth),
        along(turned(sender), nodes),
        along(turned(receiver), nodes),
        down(receiver, nodes),
    )


def first_kernel(pieces, mine, other, mesh, lend, biases, edges, sender, receiver, *rest):
    chunks, outs = rest[:-10], rest[-10:]
    sum_out, part_out, ahead_out, lent_ahead_out, lent_latent_out = outs[:5]
    outs[5][...] = through(edges[...], (mine, other), 6) + biases[2:3, :]
    ends = edge_ends(pieces, lend.shape[1], mesh.shape[0], sender[...], receiver[...])
    for out, value in zip(outs[6:], ends):
        out[...] = value
    maps = (mine, other)
    latent = mesh[...]
    part = through(latent, maps, 1).astype(BF16)
    part_out[...] = part
    ahead_out[...] = through(latent, maps, 3) + biases[1:2, :]
    lent = mm(along(turned(lend[...]), latent.shape[0]), latent).astype(BF16)
    lent_latent_out[...] = lent
    lent_ahead_out[...] = through(lent, maps, 3) + biases[1:2, :]
    sum_out[...] = encode(chunks, maps, part, biases[0:1, :])


def more_kernel(total, part, mine, other, biases, *rest):
    *chunks, out = rest
    out[...] = total[...] + encode(chunks, (mine, other), part[...], biases[0:1, :])


def last_kernel(total, part, mine, other, biases, lend, *rest):
    *chunks, out, lent_out = rest
    sums = total[...] + encode(chunks, (mine, other), part[...], biases[0:1, :])
    out[...] = sums
    lent_out[...] = rows_of(along(turned(lend[...]), sums.shape[0]), sums)


def node_kernel(lent_total, part, ahead, mine, other, biases, gains, latent, lend, *rest):
    *chunks, spread_out, notes_out, lent_out = rest
    maps = (mine, other)
    spread, notes = messages(chunks, maps, part[...], biases[0:1, :])
    spread_out[...] = spread
    notes_out[...] = notes
    lent_spread = mm(along(turned(lend[...]), spread.shape[0]), spread).astype(BF16)
    sums = ((lent_total[...] + mm(lent_spread, notes)) * gains[0:1, :]).astype(BF16)
    mid = updated(ahead[...], sums, latent[...], maps, gains)
    lent_out[...] = through(mid, maps, 7).astype(BF16)


def updated(ahead, sums, latent, maps, gains):
    hidden = silu(ahead + through(sums, maps, 4))
    change = normed(through(hidden, maps, 5)) * gains[1:2, :]
    return (latent.astype(F32) + change).astype(BF16)


def local_kernel(total, spread, notes, node_ahead, mesh, biases, gains, mine, other, *rest):
    pre, at_sender, at_receiver, mid_out, pre_out, ahead_out = rest
    maps = (mine, other)
    sums = ((total[...] + mm(spread[...], notes[...])) * gains[0:1, :]).astype(BF16)
    mid = updated(node_ahead[...], sums, mesh[...], maps, gains)
    mid_out[...] = mid
    ahead_out[...] = through(mid, maps, 10) + biases[3:4, :]
    sent = pre[...] + mm(at_sender[...], through(mid, maps, 7).astype(BF16))
    pre_out[...] = sent + mm(at_receiver[...], through(mid, maps, 8).astype(BF16))


def process_kernel(pre, ahead, picks, spread, mid, gains, mine, other, *rest):
    *lent, out = rest
    maps = (mine, other)
    table = jnp.concatenate([ref[...] for ref in lent], axis=0)
    hidden = silu(pre[...] + mm(picks[...], table))
    notes = normed(through(hidden, maps, 9)).astype(BF16)
    processed = (mm(spread[...], notes) * gains[2:3, :]).astype(BF16)
    hidden = silu(ahead[...] + through(processed, maps, 11))
    out[...] = (
        mid[...].astype(F32) + normed(through(hidden, maps, 12)) * gains[3:4, :]
    ).astype(BF16)


def call(kernel, outs, ins, specs, scratch=(), flops=0, moved=0):
    return pl.pallas_call(
        kernel,
        out_shape=[jax.ShapeDtypeStruct(shape, kind) for shape, kind in outs],
        in_specs=specs,
        out_specs=[VMEM] * len(outs),
        scratch_shapes=list(scratch),
        compiler_params=pltpu.CompilerParams(vmem_limit_bytes=VMEM_LIMIT),
        cost_estimate=pl.CostEstimate(flops=flops, bytes_accessed=moved, transcendentals=0),
    )(*ins)


def swap(value, axes, step):
    count = lax.axis_size(axes)
    return lax.ppermute(value, axes, [(i, i ^ step) for i in range(count)])


def moved(value, step):
    lats, lons = lax.axis_size("lat"), lax.axis_size("lon")
    pairs = []
    for i in range(lats * lons):
        lat, lon = (i // lons + step // lons) % lats, (i % lons + step % lons) % lons
        pairs.append((i, lat * lons + lon))
    return lax.ppermute(value, ("lat", "lon"), pairs)


def shift(value, axis, step):
    count = lax.axis_size(axis)
    return lax.ppermute(value, axis, [(i, (i + step) % count) for i in range(count)])


def paired(value, axis, first):
    count = lax.axis_size(axis)
    pairs = []
    for i in range(first, first + count, 2):
        low, high = i % count, (i + 1) % count
        pairs += [(low, high), (high, low)]
    return lax.ppermute(value, axis, pairs)


def sent_whole(chunks, owners, capacity, width):
    count = len(chunks)
    stack = jnp.stack(chunks)
    rows = stack[:, :width].reshape(count, width // LANES, LANES, LANES)
    rows = rows.transpose(0, 2, 1, 3).reshape(owners, capacity, width)
    aims = stack[:, width:].transpose(0, 2, 1).reshape(owners, capacity, AIM_ROWS)
    rows, aims = (
        lax.all_to_all(part, ("lat", "lon"), split_axis=0, concat_axis=0, tiled=True)
        for part in (rows, aims)
    )
    rows = rows.reshape(count, LANES, width // LANES, LANES).transpose(0, 2, 1, 3)
    aims = aims.reshape(count, LANES, AIM_ROWS).transpose(0, 2, 1)
    stack = jnp.concatenate([rows.reshape(count, width, LANES), aims], axis=1)
    return [stack[i] for i in range(count)]


def per_device(
    grid_latent,
    grid_owner,
    grid_target,
    mesh_latent,
    edge_latent,
    mesh_sender,
    mesh_receiver,
    halo_rows,
    weights,
    biases,
    gains,
):
    rows_dev, width = grid_latent.shape
    nodes = mesh_latent.shape[0]
    edges = edge_latent.shape[0]
    lon_count = lax.axis_size("lon")
    owners = lax.axis_size("lat") * lon_count
    capacity = max(2, 2 * rows_dev // owners)
    exchange = capacity == LANES and owners == 8

    other = swap(weights, "ch", 1)

    count = owners * capacity // LANES
    chunk_shape = ((width + AIM_ROWS, LANES), BF16)
    order = [4, 2, 6, 7, 3, 1, 5] if exchange else list(range(1, count))
    lead, place, aims = call(
        functools.partial(place_kernel, owners, capacity, exchange, order[0]),
        [chunk_shape, ((1, rows_dev), jnp.int32), ((AIM_ROWS, rows_dev), BF16)],
        [
            pltpu.with_memory_space_constraint(value, pltpu.HBM)
            for value in (grid_owner.T, grid_target.T, grid_latent)
        ],
        [HBM] * 3,
        [
            pltpu.VMEM((1, rows_dev), jnp.int32),
            pltpu.VMEM((2, rows_dev), jnp.int32),
            pltpu.VMEM((rows_dev, width), BF16),
            pltpu.SemaphoreType.DMA((3,)),
        ],
        flops=10**9,
        moved=2 * 10**6,
    )
    chunks = {order[0]: lead}
    early, late = order[1:4], [*order[4:], 0]
    for steps, after in ((early, aims), (late, other)):
        made = call(
            functools.partial(dispatch_kernel, capacity, exchange, steps),
            [chunk_shape] * len(steps),
            (place, aims, grid_latent, after),
            [VMEM] * 3 + [ANY],
            flops=10**9,
            moved=2 * 10**6,
        )
        chunks.update(zip(steps, made))
    if exchange:
        arrived = {0: chunks[0]}
        for step in order:
            arrived[step] = moved(chunks[step], step)
        groups = [[0, 4], [2, 6], [7, 3], [1], [5]]
    else:
        arrived = dict(enumerate(sent_whole([chunks[i] for i in range(count)], owners, capacity, width)))
        groups = [[0], [1], list(range(2, count))]

    depth = halo_rows.shape[0]
    lend = halo_rows.reshape(1, -1)
    pieces = 3 if lon_count == 2 else 4
    sender, receiver = mesh_sender.reshape(1, -1), mesh_receiver.reshape(1, -1)
    total, part, node_ahead, lent_ahead, lent_latent, pre, *ends = call(
        functools.partial(first_kernel, pieces),
        [((nodes, width), F32), ((nodes, width), BF16), ((nodes, width), F32)]
        + [((depth, width), F32), ((depth, width), BF16), ((edges, width), F32)]
        + [((edges, pieces * depth), BF16), ((edges, nodes), BF16)]
        + [((edges, nodes), BF16), ((nodes, edges), BF16)],
        (weights, other, mesh_latent, lend, biases, edge_latent, sender, receiver)
        + tuple(arrived[i] for i in groups[0]),
        [VMEM] * (8 + len(groups[0])),
        flops=5 * 10**8,
        moved=3 * 10**6,
    )
    for group in groups[1:-2]:
        (total,) = call(
            more_kernel,
            [((nodes, width), F32)],
            (total, part, weights, other, biases, *[arrived[i] for i in group]),
            [VMEM] * (5 + len(group)),
            flops=4 * 10**8 * len(group),
            moved=2 * 10**6,
        )
    total, lent_total = call(
        last_kernel,
        [((nodes, width), F32), ((depth, width), F32)],
        (total, part, weights, other, biases, lend, *[arrived[i] for i in groups[-2]]),
        [VMEM] * (6 + len(groups[-2])),
        flops=10**9,
        moved=2 * 10**6,
    )
    last_edges = 2 * LANES * len(groups[-1])
    spread, notes, lent = call(
        node_kernel,
        [((nodes, last_edges), BF16), ((last_edges, width), BF16), ((depth, width), BF16)],
        (lent_total, part, lent_ahead, weights, other, biases, gains, lent_latent)
        + (lend, *[arrived[i] for i in groups[-1]]),
        [VMEM] * (9 + len(groups[-1])),
        flops=10**9,
        moved=3 * 10**6,
    )
    halo = [paired(lent, "lat", 1), paired(lent, "lat", 0), shift(lent, "lon", 1)]
    if lon_count != 2:
        halo.append(shift(lent, "lon", -1))
    picks, at_sender, at_receiver, edge_spread = ends
    mid, pre, ahead = call(
        local_kernel,
        [((nodes, width), BF16), ((edges, width), F32), ((nodes, width), F32)],
        (total, spread, notes, node_ahead, mesh_latent, biases, gains, weights, other)
        + (pre, at_sender, at_receiver),
        [VMEM] * 12,
        flops=10**9,
        moved=3 * 10**6,
    )
    (out,) = call(
        process_kernel,
        [((nodes, width), BF16)],
        (pre, ahead, picks, edge_spread, mid, gains, weights, other, *halo),
        [VMEM] * (8 + pieces),
        flops=10**9,
        moved=3 * 10**6,
    )
    return out


def solution(mesh):
    in_specs = (
        P(("member", "lat", "lon", "ch"), None),
        P(("member", "lat", "lon", "ch"), None),
        P(("member", "lat", "lon", "ch"), None),
        P(("member", "lat", "lon", "ch"), None),
        P(("member", "lat", "lon", "ch"), None),
        P(("member", "lat", "lon", "ch")),
        P(("member", "lat", "lon", "ch")),
        P(("member", "lat", "lon", "ch")),
        P(None, "ch", None),
        P(),
        P(),
    )
    out_specs = P(("member", "lat", "lon", "ch"), None)
    return jax.shard_map(
        per_device, mesh=mesh, in_specs=in_specs, out_specs=out_specs, check_vma=False
    )
```

```python
import functools

import jax
import jax.numpy as jnp
from jax import lax
from jax.experimental import pallas as pl
from jax.experimental.pallas import tpu as pltpu
from jax.sharding import PartitionSpec as P

EPSILON = 1e-05
LANES = 128
AIM_ROWS = 16
F32 = jnp.float32
BF16 = jnp.bfloat16
HBM = pl.BlockSpec(memory_space=pltpu.HBM)
ANY = pl.BlockSpec(memory_space=pl.ANY)
VMEM = pl.BlockSpec(memory_space=pltpu.VMEM)
VMEM_LIMIT = 24 * 1024 * 1024


def mm(left, right):
    return jnp.dot(left, right, preferred_element_type=F32)


def mm_nt(left, right):
    return lax.dot_general(left, right, (((1,), (1,)), ((), ())), preferred_element_type=F32)


def silu(values):
    half = 0.5 * values
    return (half + half * jnp.tanh(half)).astype(BF16)


def normed(values):
    middle = jnp.mean(values, axis=-1, keepdims=True)
    centred = values - middle
    spread = jnp.mean(centred * centred, axis=-1, keepdims=True)
    return centred * lax.rsqrt(spread + EPSILON)


def as_bf16(mask):
    return jnp.where(mask, 1.0, 0.0).astype(BF16)


def down(row, count):
    return as_bf16(lax.broadcasted_iota(jnp.int32, (count, row.shape[1]), 0) == row)


def along(column, count):
    return as_bf16(lax.broadcasted_iota(jnp.int32, (column.shape[0], count), 1) == column)


def turned(row):
    wide = jnp.broadcast_to(row.astype(F32), (8, row.shape[1]))
    return jnp.transpose(wide)[:, :1].astype(jnp.int32)


def halves(rows):
    half = rows.shape[1] // 2
    low, high = rows[:, :half], rows[:, half:]
    first = lax.axis_index("ch") == 0
    return jnp.where(first, low, high), jnp.where(first, high, low)


def through(rows, maps, pick):
    here, there = halves(rows)
    return mm(here, maps[0][pick]) + mm(there, maps[1][pick])


def packed(place, aims, latent, base, out):
    rows, width = latent.shape
    pick = as_bf16(lax.broadcasted_iota(jnp.int32, (LANES, rows), 0) + base == place)
    data = mm(pick, latent).astype(BF16)
    for j in range(width // LANES):
        out[j * LANES : (j + 1) * LANES, :] = data[:, j * LANES : (j + 1) * LANES]
    out[width : width + AIM_ROWS, :] = mm_nt(aims, pick).astype(BF16)


def base_of(step, capacity, exchange):
    if not exchange:
        return step * LANES
    lats, lons = lax.axis_size("lat"), lax.axis_size("lon")
    lat, lon = lax.axis_index("lat"), lax.axis_index("lon")
    owner = lax.rem(lat + step // lons, lats) * lons + lax.rem(lon + step % lons, lons)
    return owner * capacity


def place_kernel(owners, capacity, exchange, step, owner_in, target_in, latent_in, *rest):
    out, place_out, aims_out, owner_ref, target_ref, latent_ref, sems = rest
    rows, width = latent_ref.shape
    half = rows // 2
    pairs = [(owner_in, owner_ref), (target_in, target_ref)]
    for i in range(2):
        pairs.append([ref.at[pl.ds(i * half, half), :] for ref in (latent_in, latent_ref)])
    copies = [pltpu.make_async_copy(*pair, sems.at[i]) for i, pair in enumerate(pairs)]
    for copy in copies:
        copy.start()
    number = lax.broadcasted_iota(jnp.int32, (max(16, owners), rows), 0)
    before = as_bf16(
        lax.broadcasted_iota(jnp.int32, (LANES, LANES), 0)
        < lax.broadcasted_iota(jnp.int32, (LANES, LANES), 1)
    )
    copies[0].wait()
    named = number == owner_ref[...]
    ones = jnp.where(named, 1.0, 0.0)
    ranks, ahead = [], jnp.zeros((named.shape[0], 1), F32)
    for i in range(rows // LANES):
        block = ones[:, i * LANES : (i + 1) * LANES]
        ranks.append(mm(block.astype(BF16), before) + ahead)
        ahead = ahead + jnp.sum(block, axis=1, keepdims=True)
    rank = jnp.concatenate(ranks, axis=1).astype(jnp.int32)
    place = jnp.sum(jnp.where(named, number * capacity + rank, 0), axis=0, keepdims=True)
    copies[1].wait()
    aims = jnp.concatenate(
        [
            (target_ref[...] + 1).astype(F32),
            jnp.zeros((AIM_ROWS - target_ref.shape[0], rows), F32),
        ],
        axis=0,
    ).astype(BF16)
    place_out[...] = place
    aims_out[...] = aims
    copies[2].wait()
    copies[3].wait()
    packed(place, aims, latent_ref[...], base_of(step, capacity, exchange), out)


def dispatch_kernel(capacity, exchange, steps, place_ref, aims_ref, latent_ref, after, *outs):
    del after
    place, aims, latent = place_ref[...], aims_ref[...], latent_ref[...]
    for step, out in zip(steps, outs):
        packed(place, aims, latent, base_of(step, capacity, exchange), out)


def messages(chunks, maps, mesh_part, bias):
    nodes, width = mesh_part.shape
    rows = jnp.concatenate(
        [
            jnp.concatenate(
                [chunk[j * LANES : (j + 1) * LANES, :] for j in range(width // LANES)], axis=1
            )
            for chunk in chunks
        ],
        axis=0,
    )
    lines = [chunk[width : width + AIM_ROWS, :].astype(F32) for chunk in chunks]
    columns = [jnp.transpose(line).astype(jnp.int32) - 1 for line in lines]
    lines = [line.astype(jnp.int32) - 1 for line in lines]
    part = through(rows, maps, 0) + bias
    picks = jnp.concatenate(
        [along(column[:, k : k + 1], nodes) for k in range(2) for column in columns], axis=0
    )
    spread = jnp.concatenate(
        [down(line[k : k + 1, :], nodes) for k in range(2) for line in lines], axis=1
    )
    hidden = silu(jnp.concatenate([part, part], axis=0) + mm(picks, mesh_part))
    return spread, normed(through(hidden, maps, 2)).astype(BF16)


def encode(chunks, maps, mesh_part, bias):
    return mm(*messages(chunks, maps, mesh_part, bias))


def rows_of(picks, values):
    parts = []
    for _ in range(3):
        parts.append(values.astype(BF16))
        values = values - parts[-1].astype(F32)
    return sum(mm(picks, part) for part in parts)


def edge_ends(pieces, depth, nodes, sender, receiver):
    entry = sender - nodes
    if pieces == 3:
        entry = jnp.where(entry >= 3 * depth, entry - depth, entry)
    odd = lax.rem(lax.axis_index("lat"), 2) == 1
    crossed = jnp.where(entry < 2 * depth, entry - depth, entry)
    crossed = jnp.where(entry < depth, entry + depth, crossed)
    entry = jnp.where(odd & (entry >= 0), crossed, entry)
    return (
        along(turned(entry), pieces * depth),
        along(turned(sender), nodes),
        along(turned(receiver), nodes),
        down(receiver, nodes),
    )


def first_kernel(pieces, mine, other, mesh, lend, biases, edges, sender, receiver, *rest):
    chunks, outs = rest[:-10], rest[-10:]
    sum_out, part_out, ahead_out, lent_ahead_out, lent_latent_out = outs[:5]
    outs[5][...] = through(edges[...], (mine, other), 6) + biases[2:3, :]
    ends = edge_ends(pieces, lend.shape[1], mesh.shape[0], sender[...], receiver[...])
    for out, value in zip(outs[6:], ends):
        out[...] = value
    maps = (mine, other)
    latent = mesh[...]
    part = through(latent, maps, 1).astype(BF16)
    part_out[...] = part
    ahead_out[...] = through(latent, maps, 3) + biases[1:2, :]
    lent = mm(along(turned(lend[...]), latent.shape[0]), latent).astype(BF16)
    lent_latent_out[...] = lent
    lent_ahead_out[...] = through(lent, maps, 3) + biases[1:2, :]
    sum_out[...] = encode(chunks, maps, part, biases[0:1, :])


def more_kernel(total, part, mine, other, biases, *rest):
    *chunks, out = rest
    out[...] = total[...] + encode(chunks, (mine, other), part[...], biases[0:1, :])


def last_kernel(total, part, mine, other, biases, lend, *rest):
    *chunks, out, lent_out = rest
    sums = total[...] + encode(chunks, (mine, other), part[...], biases[0:1, :])
    out[...] = sums
    lent_out[...] = rows_of(along(turned(lend[...]), sums.shape[0]), sums)


def node_kernel(lent_total, part, ahead, mine, other, biases, gains, latent, lend, *rest):
    *chunks, spread_out, notes_out, lent_out = rest
    maps = (mine, other)
    spread, notes = messages(chunks, maps, part[...], biases[0:1, :])
    spread_out[...] = spread
    notes_out[...] = notes
    lent_spread = mm(along(turned(lend[...]), spread.shape[0]), spread).astype(BF16)
    sums = ((lent_total[...] + mm(lent_spread, notes)) * gains[0:1, :]).astype(BF16)
    mid = updated(ahead[...], sums, latent[...], maps, gains)
    lent_out[...] = through(mid, maps, 7).astype(BF16)


def updated(ahead, sums, latent, maps, gains):
    hidden = silu(ahead + through(sums, maps, 4))
    change = normed(through(hidden, maps, 5)) * gains[1:2, :]
    return (latent.astype(F32) + change).astype(BF16)


def local_kernel(total, spread, notes, node_ahead, mesh, biases, gains, mine, other, *rest):
    pre, at_sender, at_receiver, mid_out, pre_out, ahead_out = rest
    maps = (mine, other)
    sums = ((total[...] + mm(spread[...], notes[...])) * gains[0:1, :]).astype(BF16)
    mid = updated(node_ahead[...], sums, mesh[...], maps, gains)
    mid_out[...] = mid
    ahead_out[...] = through(mid, maps, 10) + biases[3:4, :]
    sent = pre[...] + mm(at_sender[...], through(mid, maps, 7).astype(BF16))
    pre_out[...] = sent + mm(at_receiver[...], through(mid, maps, 8).astype(BF16))


def process_kernel(pre, ahead, picks, spread, mid, gains, mine, other, *rest):
    *lent, out = rest
    maps = (mine, other)
    table = jnp.concatenate([ref[...] for ref in lent], axis=0)
    hidden = silu(pre[...] + mm(picks[...], table))
    notes = normed(through(hidden, maps, 9)).astype(BF16)
    processed = (mm(spread[...], notes) * gains[2:3, :]).astype(BF16)
    hidden = silu(ahead[...] + through(processed, maps, 11))
    out[...] = (
        mid[...].astype(F32) + normed(through(hidden, maps, 12)) * gains[3:4, :]
    ).astype(BF16)


def call(kernel, outs, ins, specs, scratch=(), flops=0, moved=0):
    return pl.pallas_call(
        kernel,
        out_shape=[jax.ShapeDtypeStruct(shape, kind) for shape, kind in outs],
        in_specs=specs,
        out_specs=[VMEM] * len(outs),
        scratch_shapes=list(scratch),
        compiler_params=pltpu.CompilerParams(vmem_limit_bytes=VMEM_LIMIT),
        cost_estimate=pl.CostEstimate(flops=flops, bytes_accessed=moved, transcendentals=0),
    )(*ins)


def swap(value, axes, step):
    count = lax.axis_size(axes)
    return lax.ppermute(value, axes, [(i, i ^ step) for i in range(count)])


def moved(value, step):
    lats, lons = lax.axis_size("lat"), lax.axis_size("lon")
    pairs = []
    for i in range(lats * lons):
        lat, lon = (i // lons + step // lons) % lats, (i % lons + step % lons) % lons
        pairs.append((i, lat * lons + lon))
    return lax.ppermute(value, ("lat", "lon"), pairs)


def shift(value, axis, step):
    count = lax.axis_size(axis)
    return lax.ppermute(value, axis, [(i, (i + step) % count) for i in range(count)])


def paired(value, axis, first):
    count = lax.axis_size(axis)
    pairs = []
    for i in range(first, first + count, 2):
        low, high = i % count, (i + 1) % count
        pairs += [(low, high), (high, low)]
    return lax.ppermute(value, axis, pairs)


def sent_whole(chunks, owners, capacity, width):
    count = len(chunks)
    stack = jnp.stack(chunks)
    rows = stack[:, :width].reshape(count, width // LANES, LANES, LANES)
    rows = rows.transpose(0, 2, 1, 3).reshape(owners, capacity, width)
    aims = stack[:, width:].transpose(0, 2, 1).reshape(owners, capacity, AIM_ROWS)
    rows, aims = (
        lax.all_to_all(part, ("lat", "lon"), split_axis=0, concat_axis=0, tiled=True)
        for part in (rows, aims)
    )
    rows = rows.reshape(count, LANES, width // LANES, LANES).transpose(0, 2, 1, 3)
    aims = aims.reshape(count, LANES, AIM_ROWS).transpose(0, 2, 1)
    stack = jnp.concatenate([rows.reshape(count, width, LANES), aims], axis=1)
    return [stack[i] for i in range(count)]


def per_device(
    grid_latent,
    grid_owner,
    grid_target,
    mesh_latent,
    edge_latent,
    mesh_sender,
    mesh_receiver,
    halo_rows,
    weights,
    biases,
    gains,
):
    rows_dev, width = grid_latent.shape
    nodes = mesh_latent.shape[0]
    edges = edge_latent.shape[0]
    lon_count = lax.axis_size("lon")
    owners = lax.axis_size("lat") * lon_count
    capacity = max(2, 2 * rows_dev // owners)
    exchange = capacity == LANES and owners == 8

    other = swap(weights, "ch", 1)

    count = owners * capacity // LANES
    chunk_shape = ((width + AIM_ROWS, LANES), BF16)
    order = [4, 2, 6, 7, 3, 1, 5] if exchange else list(range(1, count))
    lead, place, aims = call(
        functools.partial(place_kernel, owners, capacity, exchange, order[0]),
        [chunk_shape, ((1, rows_dev), jnp.int32), ((AIM_ROWS, rows_dev), BF16)],
        [
            pltpu.with_memory_space_constraint(value, pltpu.HBM)
            for value in (grid_owner.T, grid_target.T, grid_latent)
        ],
        [HBM] * 3,
        [
            pltpu.VMEM((1, rows_dev), jnp.int32),
            pltpu.VMEM((2, rows_dev), jnp.int32),
            pltpu.VMEM((rows_dev, width), BF16),
            pltpu.SemaphoreType.DMA((4,)),
        ],
        flops=10**9,
        moved=2 * 10**6,
    )
    chunks = {order[0]: lead}
    early, late = order[1:4], [*order[4:], 0]
    for steps, after in ((early, aims), (late, other)):
        made = call(
            functools.partial(dispatch_kernel, capacity, exchange, steps),
            [chunk_shape] * len(steps),
            (place, aims, grid_latent, after),
            [VMEM] * 3 + [ANY],
            flops=10**9,
            moved=2 * 10**6,
        )
        chunks.update(zip(steps, made))
    if exchange:
        arrived = {0: chunks[0]}
        for step in order:
            arrived[step] = moved(chunks[step], step)
        groups = [[0, 4], [2, 6], [7, 3], [1], [5]]
    else:
        arrived = dict(enumerate(sent_whole([chunks[i] for i in range(count)], owners, capacity, width)))
        groups = [[0], [1], list(range(2, count))]

    depth = halo_rows.shape[0]
    lend = halo_rows.reshape(1, -1)
    pieces = 3 if lon_count == 2 else 4
    sender, receiver = mesh_sender.reshape(1, -1), mesh_receiver.reshape(1, -1)
    total, part, node_ahead, lent_ahead, lent_latent, pre, *ends = call(
        functools.partial(first_kernel, pieces),
        [((nodes, width), F32), ((nodes, width), BF16), ((nodes, width), F32)]
        + [((depth, width), F32), ((depth, width), BF16), ((edges, width), F32)]
        + [((edges, pieces * depth), BF16), ((edges, nodes), BF16)]
        + [((edges, nodes), BF16), ((nodes, edges), BF16)],
        (weights, other, mesh_latent, lend, biases, edge_latent, sender, receiver)
        + tuple(arrived[i] for i in groups[0]),
        [VMEM] * (8 + len(groups[0])),
        flops=5 * 10**8,
        moved=3 * 10**6,
    )
    for group in groups[1:-2]:
        (total,) = call(
            more_kernel,
            [((nodes, width), F32)],
            (total, part, weights, other, biases, *[arrived[i] for i in group]),
            [VMEM] * (5 + len(group)),
            flops=4 * 10**8 * len(group),
            moved=2 * 10**6,
        )
    total, lent_total = call(
        last_kernel,
        [((nodes, width), F32), ((depth, width), F32)],
        (total, part, weights, other, biases, lend, *[arrived[i] for i in groups[-2]]),
        [VMEM] * (6 + len(groups[-2])),
        flops=10**9,
        moved=2 * 10**6,
    )
    last_edges = 2 * LANES * len(groups[-1])
    spread, notes, lent = call(
        node_kernel,
        [((nodes, last_edges), BF16), ((last_edges, width), BF16), ((depth, width), BF16)],
        (lent_total, part, lent_ahead, weights, other, biases, gains, lent_latent)
        + (lend, *[arrived[i] for i in groups[-1]]),
        [VMEM] * (9 + len(groups[-1])),
        flops=10**9,
        moved=3 * 10**6,
    )
    halo = [paired(lent, "lat", 1), paired(lent, "lat", 0), shift(lent, "lon", 1)]
    if lon_count != 2:
        halo.append(shift(lent, "lon", -1))
    picks, at_sender, at_receiver, edge_spread = ends
    mid, pre, ahead = call(
        local_kernel,
        [((nodes, width), BF16), ((edges, width), F32), ((nodes, width), F32)],
        (total, spread, notes, node_ahead, mesh_latent, biases, gains, weights, other)
        + (pre, at_sender, at_receiver),
        [VMEM] * 12,
        flops=10**9,
        moved=3 * 10**6,
    )
    (out,) = call(
        process_kernel,
        [((nodes, width), BF16)],
        (pre, ahead, picks, edge_spread, mid, gains, weights, other, *halo),
        [VMEM] * (8 + pieces),
        flops=10**9,
        moved=3 * 10**6,
    )
    return out


def solution(mesh):
    in_specs = (
        P(("member", "lat", "lon", "ch"), None),
        P(("member", "lat", "lon", "ch"), None),
        P(("member", "lat", "lon", "ch"), None),
        P(("member", "lat", "lon", "ch"), None),
        P(("member", "lat", "lon", "ch"), None),
        P(("member", "lat", "lon", "ch")),
        P(("member", "lat", "lon", "ch")),
        P(("member", "lat", "lon", "ch")),
        P(None, "ch", None),
        P(),
        P(),
    )
    out_specs = P(("member", "lat", "lon", "ch"), None)
    return jax.shard_map(
        per_device, mesh=mesh, in_specs=in_specs, out_specs=out_specs, check_vma=False
    )
```

```python
import functools

import jax
import jax.numpy as jnp
from jax import lax
from jax.experimental import pallas as pl
from jax.experimental.pallas import tpu as pltpu
from jax.sharding import PartitionSpec as P

EPSILON = 1e-05
LANES = 128
AIM_ROWS = 16
F32 = jnp.float32
BF16 = jnp.bfloat16
HBM = pl.BlockSpec(memory_space=pltpu.HBM)
ANY = pl.BlockSpec(memory_space=pl.ANY)
VMEM = pl.BlockSpec(memory_space=pltpu.VMEM)
VMEM_LIMIT = 24 * 1024 * 1024


def mm(left, right):
    return jnp.dot(left, right, preferred_element_type=F32)


def mm_nt(left, right):
    return lax.dot_general(left, right, (((1,), (1,)), ((), ())), preferred_element_type=F32)


def silu(values):
    half = 0.5 * values
    return (half + half * jnp.tanh(half)).astype(BF16)


def normed(values):
    middle = jnp.mean(values, axis=-1, keepdims=True)
    centred = values - middle
    spread = jnp.mean(centred * centred, axis=-1, keepdims=True)
    return centred * lax.rsqrt(spread + EPSILON)


def as_bf16(mask):
    return jnp.where(mask, 1.0, 0.0).astype(BF16)


def down(row, count):
    return as_bf16(lax.broadcasted_iota(jnp.int32, (count, row.shape[1]), 0) == row)


def along(column, count):
    return as_bf16(lax.broadcasted_iota(jnp.int32, (column.shape[0], count), 1) == column)


def turned(row):
    wide = jnp.broadcast_to(row.astype(F32), (8, row.shape[1]))
    return jnp.transpose(wide)[:, :1].astype(jnp.int32)


def halves(rows):
    half = rows.shape[1] // 2
    low, high = rows[:, :half], rows[:, half:]
    first = lax.axis_index("ch") == 0
    return jnp.where(first, low, high), jnp.where(first, high, low)


def through(rows, maps, pick):
    here, there = halves(rows)
    return mm(here, maps[0][pick]) + mm(there, maps[1][pick])


def packed(place, aims, latent, base, out):
    rows, width = latent.shape
    pick = as_bf16(lax.broadcasted_iota(jnp.int32, (LANES, rows), 0) + base == place)
    data = mm(pick, latent).astype(BF16)
    for j in range(width // LANES):
        out[j * LANES : (j + 1) * LANES, :] = data[:, j * LANES : (j + 1) * LANES]
    out[width : width + AIM_ROWS, :] = mm_nt(aims, pick).astype(BF16)


def base_of(step, capacity, exchange):
    if not exchange:
        return step * LANES
    lats, lons = lax.axis_size("lat"), lax.axis_size("lon")
    lat, lon = lax.axis_index("lat"), lax.axis_index("lon")
    owner = lax.rem(lat + step // lons, lats) * lons + lax.rem(lon + step % lons, lons)
    return owner * capacity


def place_kernel(owners, capacity, exchange, step, owner_in, target_in, latent_in, *rest):
    out, place_out, aims_out, owner_ref, target_ref, latent_ref, sems = rest
    rows, width = latent_ref.shape
    pairs = ((owner_in, owner_ref), (target_in, target_ref), (latent_in, latent_ref))
    copies = [pltpu.make_async_copy(*pair, sems.at[i]) for i, pair in enumerate(pairs)]
    for copy in copies:
        copy.start()
    number = lax.broadcasted_iota(jnp.int32, (max(16, owners), rows), 0)
    before = as_bf16(
        lax.broadcasted_iota(jnp.int32, (rows, rows), 0)
        < lax.broadcasted_iota(jnp.int32, (rows, rows), 1)
    )
    copies[0].wait()
    named = number == owner_ref[...]
    rank = mm(as_bf16(named), before).astype(jnp.int32)
    place = jnp.sum(jnp.where(named, number * capacity + rank, 0), axis=0, keepdims=True)
    copies[1].wait()
    aims = jnp.concatenate(
        [
            (target_ref[...] + 1).astype(F32),
            jnp.zeros((AIM_ROWS - target_ref.shape[0], rows), F32),
        ],
        axis=0,
    ).astype(BF16)
    place_out[...] = place
    aims_out[...] = aims
    copies[2].wait()
    packed(place, aims, latent_ref[...], base_of(step, capacity, exchange), out)


def dispatch_kernel(capacity, exchange, steps, place_ref, aims_ref, latent_ref, after, *outs):
    del after
    place, aims, latent = place_ref[...], aims_ref[...], latent_ref[...]
    for step, out in zip(steps, outs):
        packed(place, aims, latent, base_of(step, capacity, exchange), out)


def messages(chunks, maps, mesh_part, bias):
    nodes, width = mesh_part.shape
    rows = jnp.concatenate(
        [
            jnp.concatenate(
                [chunk[j * LANES : (j + 1) * LANES, :] for j in range(width // LANES)], axis=1
            )
            for chunk in chunks
        ],
        axis=0,
    )
    lines = [chunk[width : width + AIM_ROWS, :].astype(F32) for chunk in chunks]
    columns = [jnp.transpose(line).astype(jnp.int32) - 1 for line in lines]
    lines = [line.astype(jnp.int32) - 1 for line in lines]
    part = through(rows, maps, 0) + bias
    picks = jnp.concatenate(
        [along(column[:, k : k + 1], nodes) for k in range(2) for column in columns], axis=0
    )
    spread = jnp.concatenate(
        [down(line[k : k + 1, :], nodes) for k in range(2) for line in lines], axis=1
    )
    hidden = silu(jnp.concatenate([part, part], axis=0) + mm(picks, mesh_part))
    return spread, normed(through(hidden, maps, 2)).astype(BF16)


def encode(chunks, maps, mesh_part, bias):
    return mm(*messages(chunks, maps, mesh_part, bias))


def rows_of(picks, values):
    parts = []
    for _ in range(3):
        parts.append(values.astype(BF16))
        values = values - parts[-1].astype(F32)
    return sum(mm(picks, part) for part in parts)


def edge_ends(pieces, depth, nodes, sender, receiver):
    entry = sender - nodes
    if pieces == 3:
        entry = jnp.where(entry >= 3 * depth, entry - depth, entry)
    odd = lax.rem(lax.axis_index("lat"), 2) == 1
    crossed = jnp.where(entry < 2 * depth, entry - depth, entry)
    crossed = jnp.where(entry < depth, entry + depth, crossed)
    entry = jnp.where(odd & (entry >= 0), crossed, entry)
    return (
        along(turned(entry), pieces * depth),
        along(turned(sender), nodes),
        along(turned(receiver), nodes),
        down(receiver, nodes),
    )


def first_kernel(pieces, mine, other, mesh, lend, biases, edges, sender, receiver, *rest):
    chunks, outs = rest[:-10], rest[-10:]
    sum_out, part_out, ahead_out, lent_ahead_out, lent_latent_out = outs[:5]
    outs[5][...] = through(edges[...], (mine, other), 6) + biases[2:3, :]
    ends = edge_ends(pieces, lend.shape[1], mesh.shape[0], sender[...], receiver[...])
    for out, value in zip(outs[6:], ends):
        out[...] = value
    maps = (mine, other)
    latent = mesh[...]
    part = through(latent, maps, 1).astype(BF16)
    part_out[...] = part
    ahead_out[...] = through(latent, maps, 3) + biases[1:2, :]
    lent = mm(along(turned(lend[...]), latent.shape[0]), latent).astype(BF16)
    lent_latent_out[...] = lent
    lent_ahead_out[...] = through(lent, maps, 3) + biases[1:2, :]
    sum_out[...] = encode(chunks, maps, part, biases[0:1, :])


def more_kernel(total, part, mine, other, biases, *rest):
    *chunks, out = rest
    out[...] = total[...] + encode(chunks, (mine, other), part[...], biases[0:1, :])


def last_kernel(total, part, mine, other, biases, lend, *rest):
    *chunks, out, lent_out = rest
    sums = total[...] + encode(chunks, (mine, other), part[...], biases[0:1, :])
    out[...] = sums
    lent_out[...] = rows_of(along(turned(lend[...]), sums.shape[0]), sums)


def node_kernel(lent_total, part, ahead, mine, other, biases, gains, latent, lend, *rest):
    *chunks, spread_out, notes_out, lent_out = rest
    maps = (mine, other)
    spread, notes = messages(chunks, maps, part[...], biases[0:1, :])
    spread_out[...] = spread
    notes_out[...] = notes
    lent_spread = mm(along(turned(lend[...]), spread.shape[0]), spread).astype(BF16)
    sums = ((lent_total[...] + mm(lent_spread, notes)) * gains[0:1, :]).astype(BF16)
    mid = updated(ahead[...], sums, latent[...], maps, gains)
    lent_out[...] = through(mid, maps, 7).astype(BF16)


def updated(ahead, sums, latent, maps, gains):
    hidden = silu(ahead + through(sums, maps, 4))
    change = normed(through(hidden, maps, 5)) * gains[1:2, :]
    return (latent.astype(F32) + change).astype(BF16)


def local_kernel(total, spread, notes, node_ahead, mesh, biases, gains, mine, other, *rest):
    pre, at_sender, at_receiver, mid_out, pre_out, ahead_out = rest
    maps = (mine, other)
    sums = ((total[...] + mm(spread[...], notes[...])) * gains[0:1, :]).astype(BF16)
    mid = updated(node_ahead[...], sums, mesh[...], maps, gains)
    mid_out[...] = mid
    ahead_out[...] = through(mid, maps, 10) + biases[3:4, :]
    sent = pre[...] + mm(at_sender[...], through(mid, maps, 7).astype(BF16))
    pre_out[...] = sent + mm(at_receiver[...], through(mid, maps, 8).astype(BF16))


def process_kernel(pre, ahead, picks, spread, mid, gains, mine, other, *rest):
    *lent, out = rest
    lent = [lent[0], lent[-1], *lent[1:-1]]
    maps = (mine, other)
    table = jnp.concatenate([ref[...] for ref in lent], axis=0)
    hidden = silu(pre[...] + mm(picks[...], table))
    notes = normed(through(hidden, maps, 9)).astype(BF16)
    processed = (mm(spread[...], notes) * gains[2:3, :]).astype(BF16)
    hidden = silu(ahead[...] + through(processed, maps, 11))
    out[...] = (
        mid[...].astype(F32) + normed(through(hidden, maps, 12)) * gains[3:4, :]
    ).astype(BF16)


def call(kernel, outs, ins, specs, scratch=(), flops=0, moved=0):
    return pl.pallas_call(
        kernel,
        out_shape=[jax.ShapeDtypeStruct(shape, kind) for shape, kind in outs],
        in_specs=specs,
        out_specs=[VMEM] * len(outs),
        scratch_shapes=list(scratch),
        compiler_params=pltpu.CompilerParams(vmem_limit_bytes=VMEM_LIMIT),
        cost_estimate=pl.CostEstimate(flops=flops, bytes_accessed=moved, transcendentals=0),
    )(*ins)


def swap(value, axes, step):
    count = lax.axis_size(axes)
    return lax.ppermute(value, axes, [(i, i ^ step) for i in range(count)])


def moved(value, step):
    lats, lons = lax.axis_size("lat"), lax.axis_size("lon")
    pairs = []
    for i in range(lats * lons):
        lat, lon = (i // lons + step // lons) % lats, (i % lons + step % lons) % lons
        pairs.append((i, lat * lons + lon))
    return lax.ppermute(value, ("lat", "lon"), pairs)


def shift(value, axis, step):
    count = lax.axis_size(axis)
    return lax.ppermute(value, axis, [(i, (i + step) % count) for i in range(count)])


def paired(value, axis, first):
    count = lax.axis_size(axis)
    pairs = []
    for i in range(first, first + count, 2):
        low, high = i % count, (i + 1) % count
        pairs += [(low, high), (high, low)]
    return lax.ppermute(value, axis, pairs)


def sent_whole(chunks, owners, capacity, width):
    count = len(chunks)
    stack = jnp.stack(chunks)
    rows = stack[:, :width].reshape(count, width // LANES, LANES, LANES)
    rows = rows.transpose(0, 2, 1, 3).reshape(owners, capacity, width)
    aims = stack[:, width:].transpose(0, 2, 1).reshape(owners, capacity, AIM_ROWS)
    rows, aims = (
        lax.all_to_all(part, ("lat", "lon"), split_axis=0, concat_axis=0, tiled=True)
        for part in (rows, aims)
    )
    rows = rows.reshape(count, LANES, width // LANES, LANES).transpose(0, 2, 1, 3)
    aims = aims.reshape(count, LANES, AIM_ROWS).transpose(0, 2, 1)
    stack = jnp.concatenate([rows.reshape(count, width, LANES), aims], axis=1)
    return [stack[i] for i in range(count)]


def per_device(
    grid_latent,
    grid_owner,
    grid_target,
    mesh_latent,
    edge_latent,
    mesh_sender,
    mesh_receiver,
    halo_rows,
    weights,
    biases,
    gains,
):
    rows_dev, width = grid_latent.shape
    nodes = mesh_latent.shape[0]
    edges = edge_latent.shape[0]
    lon_count = lax.axis_size("lon")
    owners = lax.axis_size("lat") * lon_count
    capacity = max(2, 2 * rows_dev // owners)
    exchange = capacity == LANES and owners == 8

    other = swap(weights, "ch", 1)

    count = owners * capacity // LANES
    chunk_shape = ((width + AIM_ROWS, LANES), BF16)
    order = [4, 2, 6, 7, 3, 1, 5] if exchange else list(range(1, count))
    lead, place, aims = call(
        functools.partial(place_kernel, owners, capacity, exchange, order[0]),
        [chunk_shape, ((1, rows_dev), jnp.int32), ((AIM_ROWS, rows_dev), BF16)],
        [
            pltpu.with_memory_space_constraint(value, pltpu.HBM)
            for value in (grid_owner.T, grid_target.T, grid_latent)
        ],
        [HBM] * 3,
        [
            pltpu.VMEM((1, rows_dev), jnp.int32),
            pltpu.VMEM((2, rows_dev), jnp.int32),
            pltpu.VMEM((rows_dev, width), BF16),
            pltpu.SemaphoreType.DMA((3,)),
        ],
        flops=10**9,
        moved=2 * 10**6,
    )
    chunks = {order[0]: lead}
    early, late = order[1:4], [*order[4:], 0]
    for steps, after in ((early, aims), (late, other)):
        made = call(
            functools.partial(dispatch_kernel, capacity, exchange, steps),
            [chunk_shape] * len(steps),
            (place, aims, grid_latent, after),
            [VMEM] * 3 + [ANY],
            flops=10**9,
            moved=2 * 10**6,
        )
        chunks.update(zip(steps, made))
    if exchange:
        arrived = {0: chunks[0]}
        for step in order:
            arrived[step] = moved(chunks[step], step)
        groups = [[0, 4], [2, 6], [7, 3], [1], [5]]
    else:
        arrived = dict(enumerate(sent_whole([chunks[i] for i in range(count)], owners, capacity, width)))
        groups = [[0], [1], list(range(2, count))]

    depth = halo_rows.shape[0]
    lend = halo_rows.reshape(1, -1)
    pieces = 3 if lon_count == 2 else 4
    sender, receiver = mesh_sender.reshape(1, -1), mesh_receiver.reshape(1, -1)
    total, part, node_ahead, lent_ahead, lent_latent, pre, *ends = call(
        functools.partial(first_kernel, pieces),
        [((nodes, width), F32), ((nodes, width), BF16), ((nodes, width), F32)]
        + [((depth, width), F32), ((depth, width), BF16), ((edges, width), F32)]
        + [((edges, pieces * depth), BF16), ((edges, nodes), BF16)]
        + [((edges, nodes), BF16), ((nodes, edges), BF16)],
        (weights, other, mesh_latent, lend, biases, edge_latent, sender, receiver)
        + tuple(arrived[i] for i in groups[0]),
        [VMEM] * (8 + len(groups[0])),
        flops=5 * 10**8,
        moved=3 * 10**6,
    )
    for group in groups[1:-2]:
        (total,) = call(
            more_kernel,
            [((nodes, width), F32)],
            (total, part, weights, other, biases, *[arrived[i] for i in group]),
            [VMEM] * (5 + len(group)),
            flops=4 * 10**8 * len(group),
            moved=2 * 10**6,
        )
    total, lent_total = call(
        last_kernel,
        [((nodes, width), F32), ((depth, width), F32)],
        (total, part, weights, other, biases, lend, *[arrived[i] for i in groups[-2]]),
        [VMEM] * (6 + len(groups[-2])),
        flops=10**9,
        moved=2 * 10**6,
    )
    last_edges = 2 * LANES * len(groups[-1])
    spread, notes, lent = call(
        node_kernel,
        [((nodes, last_edges), BF16), ((last_edges, width), BF16), ((depth, width), BF16)],
        (lent_total, part, lent_ahead, weights, other, biases, gains, lent_latent)
        + (lend, *[arrived[i] for i in groups[-1]]),
        [VMEM] * (9 + len(groups[-1])),
        flops=10**9,
        moved=3 * 10**6,
    )
    halo = [paired(lent, "lat", 1), paired(lent, "lat", 0), shift(lent, "lon", 1)]
    if lon_count != 2:
        halo.append(shift(lent, "lon", -1))
    picks, at_sender, at_receiver, edge_spread = ends
    mid, pre, ahead = call(
        local_kernel,
        [((nodes, width), BF16), ((edges, width), F32), ((nodes, width), F32)],
        (total, spread, notes, node_ahead, mesh_latent, biases, gains, weights, other)
        + (pre, at_sender, at_receiver),
        [VMEM] * 12,
        flops=10**9,
        moved=3 * 10**6,
    )
    (out,) = call(
        process_kernel,
        [((nodes, width), BF16)],
        (pre, ahead, picks, edge_spread, mid, gains, weights, other, halo[0], *halo[2:], halo[1]),
        [VMEM] * (8 + pieces),
        flops=10**9,
        moved=3 * 10**6,
    )
    return out


def solution(mesh):
    in_specs = (
        P(("member", "lat", "lon", "ch"), None),
        P(("member", "lat", "lon", "ch"), None),
        P(("member", "lat", "lon", "ch"), None),
        P(("member", "lat", "lon", "ch"), None),
        P(("member", "lat", "lon", "ch"), None),
        P(("member", "lat", "lon", "ch")),
        P(("member", "lat", "lon", "ch")),
        P(("member", "lat", "lon", "ch")),
        P(None, "ch", None),
        P(),
        P(),
    )
    out_specs = P(("member", "lat", "lon", "ch"), None)
    return jax.shard_map(
        per_device, mesh=mesh, in_specs=in_specs, out_specs=out_specs, check_vma=False
    )
```
